32 devices in a mesh: comp: 2 (over core), blk: 16 (over z, y, x).
Axes of the slice: x: 2, y: 2, z: 4, core: 2. Of those that a mesh axis runs over, the one named last changes fastest.
Arguments:
- thermal_profiles: float32 [2, 80, 131072], P('comp', None, 'blk'), may hold values from -6 to 6
- adjacent_positions: int32 [2, 6, 131072], P('comp', None, 'blk'), may hold values from 0 to 10239
- diffusion_link_factor: float32 [2, 6, 131072], P('comp', None, 'blk'), may hold values from 0.01 to 0.15
- implicit_solver_matrix: float32 [2, 80, 80], P('comp'), may hold values from -0.6 to 1.2
- lagged_surface_temp: float32 [131072], P('blk'), may hold values from -6 to 6
- flux_coefficient: float32 [16, 131072], P(None, 'blk'), may hold values from 0.2 to 2
- flux_heating: float32 [16], replicated, may hold values from -3 to 3
- ocean_cell_mask: int32 [131072], P('blk'), may hold values 0 or 1
- atmosphere_slot_cells: int32 [16, 16, 256], P('blk'), may hold values from 0 to 8191
- ocean_slot_cells: int32 [16, 16, 512], P('blk'), may hold values from 0 to 8191
- forward_weight_blocks: float32 [16, 16, 512, 256], P('blk'), may hold values from -0.375 to 0.375
- backward_weight_blocks: float32 [16, 16, 256, 512], P('blk'), may hold values from -0.25 to 0.25
Outputs:
- partition_thermal_result: float32 [2, 80, 131072], P('comp', None, 'blk')
- interface_exchange_values: float32 [2, 16, 131072], P('comp', None, 'blk')
- interface_warmth_values: float32 [2, 131072], P('comp', 'blk')
The draws below stay inside these ranges and needn't reach their ends.
All inputs are finite; a program needn't handle non-finite values. No bound on the sum of `ocean_cell_mask` on one device may be relied on, other than what follows from the above.
Results may differ from the reference program's by a relative error of at most 0.0001.
Values sent between devices are 32-bit elements; how exact they have to be, the bound alone decides.
No kernel may reach another device: no remote copies, remote signals or barrier semaphores. Data moves between devices by JAX's collectives and lax.ppermute only.
A program may use at most 128 MiB of HBM per device.

```python
import math
import jax
import jax.numpy as jnp
from jax import lax

OWNER_CELLS = 8192
VERTICAL_LEVELS = 80
NBR = 6
NF = 16
SECTION_CELLS = 131072
KA = 256
OCEAN_SLOTS = 512
HALO = 1024
N_BLK = 16


def draw_implicit_solver_matrix(key, part):
    noise = jnp.clip(jax.random.normal(key, (2, VERTICAL_LEVELS, VERTICAL_LEVELS), jnp.float32), -4.0, 4.0)
    identity = (jnp.arange(VERTICAL_LEVELS)[:, None] == jnp.arange(VERTICAL_LEVELS)[None, :]).astype(jnp.float32)
    return 0.6 * identity[None, :, :] + 0.4 / math.sqrt(VERTICAL_LEVELS) * noise


def place_ends(result, rng, smallest, largest):
    longest = result.shape.index(max(result.shape))
    spots = []
    for shift in (0, 1):
        where = [jax.random.randint(jax.random.fold_in(rng, axis), (), 0, length) for axis, length in enumerate(result.shape)]
        where[longest] = (where[longest] + shift) % result.shape[longest]
        spots.append(tuple(where))
    return result.at[spots[0]].set(smallest).at[spots[1]].set(largest)


def level_of(key, shape, pieces, smallest, high):
    def one(axis_at, shards_of):
        steps = jax.random.uniform(jax.random.fold_in(jax.random.fold_in(key, 6), axis_at), (shards_of,), jnp.float32, smallest / len(pieces), high / len(pieces))
        return jnp.repeat(jnp.exp(steps), shape[axis_at] // shards_of).reshape((-1,) + (1,) * (len(shape) - axis_at - 1))

    factor_of = one(*pieces[0])
    for cut in pieces[1:]:
        factor_of = factor_of * one(*cut)
    return factor_of


def normal_values(own_key, dims, spread, most, split=(), dtype=jnp.bfloat16):
    drawn = jax.random.normal(own_key, dims, jnp.float32) * spread
    if len(split) > 0:
        drawn = level_of(own_key, dims, split, -0.22, 0.18) * drawn
    return jnp.clip(drawn, min=-most, max=most).astype(dtype)


def setup_inputs(seed: int = 0) -> dict:
    keys = jax.random.split(jax.random.key(seed), 13)
    thermal_profiles = normal_values(keys[0], (2, VERTICAL_LEVELS, SECTION_CELLS), 1.0, 6.0, ((0, 2), (2, 16)), jnp.float32)
    adjacent_positions = place_ends(jax.random.randint(keys[1], (2, NBR, SECTION_CELLS), 0, OWNER_CELLS + 2 * HALO), jax.random.fold_in(keys[1], 1), 0, (OWNER_CELLS + 2 * HALO) - 1).astype(jnp.int32)
    diffusion_link_factor = jnp.clip(jnp.exp(math.log(0.15) - 2.7080503 * jax.random.uniform(keys[2], (2, NBR, SECTION_CELLS), jnp.float32) ** level_of(keys[2], (2, NBR, SECTION_CELLS), ((0, 2), (2, 16)), -0.2, 0.2)), 0.01, 0.15)
    implicit_solver_matrix = draw_implicit_solver_matrix(jax.random.fold_in(keys[12], 71), 0)
    lagged_surface_temp = normal_values(keys[4], (SECTION_CELLS,), 1.0, 6.0, ((0, 16),), jnp.float32)
    flux_coefficient = jnp.clip(jnp.exp(math.log(2.0) - 2.3025851 * jax.random.uniform(keys[5], (NF, SECTION_CELLS), jnp.float32) ** level_of(keys[5], (NF, SECTION_CELLS), ((1, 16),), -0.2, 0.2)), 0.2, 2.0)
    flux_heating = normal_values(keys[6], (NF,), 0.5, 3.0, (), jnp.float32)
    ocean_cell_mask = place_ends((jax.random.randint(keys[7], (SECTION_CELLS,), 0, 10) < 7).astype(jnp.int32), jax.random.fold_in(keys[7], 1), 0, 1)
    atmosphere_slot_cells = place_ends(jax.random.randint(keys[8], (N_BLK, N_BLK, KA), 0, OWNER_CELLS), jax.random.fold_in(keys[8], 1), 0, OWNER_CELLS - 1).astype(jnp.int32)
    ocean_slot_cells = place_ends(jax.random.randint(keys[9], (N_BLK, N_BLK, OCEAN_SLOTS), 0, OWNER_CELLS), jax.random.fold_in(keys[9], 1), 0, OWNER_CELLS - 1).astype(jnp.int32)
    forward_weight_blocks = normal_values(keys[10], (N_BLK, N_BLK, OCEAN_SLOTS, KA), KA ** -0.5, 0.375, ((0, 16),), jnp.float32)
    backward_weight_blocks = normal_values(keys[11], (N_BLK, N_BLK, KA, OCEAN_SLOTS), OCEAN_SLOTS ** -0.5, 0.25, ((0, 16),), jnp.float32)
    return dict(thermal_profiles=thermal_profiles, adjacent_positions=adjacent_positions, diffusion_link_factor=diffusion_link_factor, implicit_solver_matrix=implicit_solver_matrix, lagged_surface_temp=lagged_surface_temp, flux_coefficient=flux_coefficient, flux_heating=flux_heating, ocean_cell_mask=ocean_cell_mask, atmosphere_slot_cells=atmosphere_slot_cells, ocean_slot_cells=ocean_slot_cells, forward_weight_blocks=forward_weight_blocks, backward_weight_blocks=backward_weight_blocks)


def advance_partition(field_now, nearby, edge_w, solver):
    blocks = field_now.reshape(VERTICAL_LEVELS, N_BLK, OWNER_CELLS)
    before_rim = jnp.roll(blocks[:, :, OWNER_CELLS - HALO:], 1, axis=1)
    after_rim = jnp.roll(blocks[:, :, :HALO], -1, axis=1)
    extended = jnp.concatenate([before_rim, blocks, after_rim], axis=2)
    near_blocks = nearby.reshape(NBR, N_BLK, OWNER_CELLS)
    weight_blocks = edge_w.reshape(NBR, N_BLK, OWNER_CELLS)
    change = jnp.zeros_like(blocks)
    for j in range(NBR):
        where_from = jnp.broadcast_to(near_blocks[j][None], blocks.shape).astype(jnp.int32)
        picked = jnp.take_along_axis(extended, where_from, axis=2)
        change = change + weight_blocks[j][None] * (picked - blocks)
    updated = (blocks + change).reshape(VERTICAL_LEVELS, N_BLK * OWNER_CELLS)
    return jnp.dot(solver, updated, precision=lax.Precision.HIGHEST)


def pack_atm(flux_rows, slot_row_list):
    return jnp.take(flux_rows, slot_row_list.reshape(-1), axis=0).reshape(N_BLK, KA, NF)


def scatter_ocean(mapped_rows, slot_row_list):
    empty = jnp.zeros((OWNER_CELLS, NF), jnp.float32)
    return empty.at[slot_row_list.reshape(-1)].add(mapped_rows.reshape(N_BLK * OCEAN_SLOTS, NF))


def gather_ocean_rows(surface_temp_rows, slot_row_list):
    return jnp.take(surface_temp_rows, slot_row_list.reshape(-1), axis=0).reshape(N_BLK, OCEAN_SLOTS)


def spread_atmosphere(mapped_rows, slot_row_list):
    empty = jnp.zeros((OWNER_CELLS,), jnp.float32)
    return empty.at[slot_row_list.reshape(-1)].add(mapped_rows.reshape(-1))


def reference(thermal_profiles, adjacent_positions, diffusion_link_factor, implicit_solver_matrix, lagged_surface_temp, flux_coefficient, flux_heating, ocean_cell_mask, atmosphere_slot_cells, ocean_slot_cells, forward_weight_blocks, backward_weight_blocks):
    water_indicator = ocean_cell_mask.astype(jnp.float32)
    atmosphere_flux = flux_coefficient * (thermal_profiles[0, VERTICAL_LEVELS - 1] - lagged_surface_temp)[None, :]
    atm_rows = atmosphere_flux.T.reshape(N_BLK, OWNER_CELLS, NF)
    packed = jax.vmap(pack_atm)(atm_rows, atmosphere_slot_cells)
    mapped = jnp.einsum("oajk,aokf->oajf", forward_weight_blocks, packed, precision=lax.Precision.HIGHEST)
    ocean_rows = jax.vmap(scatter_ocean)(mapped, ocean_slot_cells)
    ocean_flux = ocean_rows.reshape(N_BLK * OWNER_CELLS, NF).T * water_indicator[None, :]
    driving_source = jnp.sum(flux_heating[:, None] * ocean_flux, axis=0)
    air_profile_now = thermal_profiles[0]
    marine_thermal_profile = thermal_profiles[1].at[0].add(driving_source)
    for step in range(2):
        air_profile_now = advance_partition(air_profile_now, adjacent_positions[0], diffusion_link_factor[0], implicit_solver_matrix[0])
        marine_thermal_profile = advance_partition(marine_thermal_profile, adjacent_positions[1], diffusion_link_factor[1], implicit_solver_matrix[1])
    sea_skin_warmth = marine_thermal_profile[0] * water_indicator
    return_rows = jax.vmap(gather_ocean_rows)(sea_skin_warmth.reshape(N_BLK, OWNER_CELLS), ocean_slot_cells)
    remapped_return = jnp.einsum("aokj,oaj->aok", backward_weight_blocks, return_rows, precision=lax.Precision.HIGHEST)
    atmosphere_surface_temp = jax.vmap(spread_atmosphere)(remapped_return, atmosphere_slot_cells).reshape(N_BLK * OWNER_CELLS)
    partition_thermal_result = jnp.stack([air_profile_now, marine_thermal_profile])
    interface_exchange_values = jnp.stack([atmosphere_flux, ocean_flux])
    interface_warmth_values = jnp.stack([atmosphere_surface_temp, sea_skin_warmth])
    return (partition_thermal_result, interface_exchange_values, interface_warmth_values)
```

```python
import functools

import jax
import jax.numpy as jnp
from jax import lax
from jax.experimental import pallas as pl
from jax.experimental.pallas import tpu as pltpu
from jax.sharding import PartitionSpec as P

HALO = 1024
CHUNK = 128
LANES = 128
SUB = 8
BUFFERS = 4
LIMIT = 56 * 2**20
HIGHEST = lax.Precision.HIGHEST


def to_rows_kernel(field_ref, forcing_ref, rows_ref):
    levels, width = field_ref.shape
    level = lax.broadcasted_iota(jnp.int32, (SUB, LANES), 0)
    for k in range(width // LANES):
        cut = slice(k * LANES, (k + 1) * LANES)
        forcing = jnp.where(level == 0, jnp.broadcast_to(forcing_ref[:, cut], (SUB, LANES)), 0.0)
        block = jnp.concatenate(
            [
                field_ref[:SUB, cut] + forcing,
                field_ref[SUB:, cut],
                jnp.zeros((LANES - levels, LANES), jnp.float32),
            ],
            axis=0,
        )
        rows_ref[cut, :] = block.T


def to_rows(field, forcing, width=1024):
    levels, cells = field.shape
    width = min(width, cells)
    return pl.pallas_call(
        to_rows_kernel,
        grid=(cells // width,),
        in_specs=[
            pl.BlockSpec((levels, width), lambda i: (0, i)),
            pl.BlockSpec((1, width), lambda i: (0, i)),
        ],
        out_specs=pl.BlockSpec((width, LANES), lambda i: (i, 0)),
        out_shape=jax.ShapeDtypeStruct((cells, LANES), jnp.float32),
        compiler_params=pltpu.CompilerParams(vmem_limit_bytes=LIMIT),
        name="to_rows",
    )(field, forcing)


def split(value):
    high = value.astype(jnp.bfloat16)
    return high, (value - high.astype(jnp.float32)).astype(jnp.bfloat16)


def dot_nt(a, b):
    return lax.dot_general(a, b, (((1,), (1,)), ((), ())), preferred_element_type=jnp.float32)


def mix_kernel(pieces, first_chunk, solve, *refs):
    count = len(pieces)
    piece_refs, refs = refs[:count], refs[count:]
    if solve:
        solver_ref, refs = refs[0], refs[1:]
    near_ref, edge_ref, out_ref, table, *slots, near_sems, piece_sems = refs
    neighbours = near_ref.shape[0]
    chunks = out_ref.shape[1 if solve else 0] // CHUNK

    def fetch(i, slot):
        start = pl.multiple_of(first_chunk(i) * CHUNK, CHUNK)
        return pltpu.make_async_copy(
            near_ref.at[:, :, pl.ds(start, CHUNK)], slots[slot], near_sems.at[slot]
        )

    loads = [
        pltpu.make_async_copy(
            ref.at[pl.ds(row, length)], table.at[pl.ds(start, length)], piece_sems.at[k]
        )
        for k, (ref, row, start, length) in enumerate(
            (piece_refs[k], row, start, length) for k, (row, start, length) in enumerate(pieces)
        )
    ]
    for load in loads:
        load.start()
    for slot in range(BUFFERS - 1):
        fetch(slot, slot).start()
    for load in loads:
        load.wait()
    lane_sub = lax.broadcasted_iota(jnp.int32, (SUB, LANES), 0)
    masks = [lane_sub == s for s in range(SUB)]

    def body(turn, carry):
        for slot in range(BUFFERS):
            i = turn * BUFFERS + slot
            fetch(i, slot).wait()

            @pl.when(i + BUFFERS - 1 < chunks)
            def _():
                fetch(i + BUFFERS - 1, (slot + BUFFERS - 1) % BUFFERS).start()

            cell = pl.multiple_of(first_chunk(i) * CHUNK, CHUNK)
            edges = [edge_ref[j, :, pl.ds(cell, CHUNK)] for j in range(neighbours)]
            keep = 1.0 - functools.reduce(lambda a, b: a + b, edges)
            stacked = jnp.concatenate(
                edges + [keep, jnp.zeros((SUB - neighbours - 1, CHUNK), jnp.float32)], axis=0
            )
            factors = stacked.T
            mixed = []
            for g in range(CHUNK // SUB):
                own = table[pl.ds(pl.multiple_of(HALO + cell + g * SUB, SUB), SUB), :]
                part = factors[g * SUB : (g + 1) * SUB]
                total = jnp.broadcast_to(part[:, neighbours : neighbours + 1], (SUB, LANES)) * own
                for j in range(neighbours):
                    picked = None
                    for s in range(SUB):
                        where = slots[slot][j, 0, g * SUB + s]
                        row = jnp.broadcast_to(table[pl.ds(where, 1), :], (SUB, LANES))
                        picked = row if s == 0 else jnp.where(masks[s], row, picked)
                    total = total + jnp.broadcast_to(part[:, j : j + 1], (SUB, LANES)) * picked
                if solve:
                    mixed.append(total)
                else:
                    out_ref[pl.ds(pl.multiple_of(i * CHUNK + g * SUB, SUB), SUB), :] = total
            if solve:
                high, low = split(jnp.concatenate(mixed, axis=0))
                solver_high, solver_low = split(solver_ref[...])
                out_ref[:, pl.ds(pl.multiple_of(i * CHUNK, CHUNK), CHUNK)] = (
                    dot_nt(solver_high, low) + dot_nt(solver_low, high)
                ) + dot_nt(solver_high, high)
        return carry

    lax.fori_loop(0, chunks // BUFFERS, body, 0)


def mix(pieces, near, edges, chunk_of, chunks, solver=None):
    rows = sum(length for _, _, _, length in pieces)
    anywhere = pl.BlockSpec(memory_space=pl.ANY)
    solve = solver is not None
    if solve:
        out_shape = jax.ShapeDtypeStruct((solver.shape[0], chunks * CHUNK), jnp.float32)
    else:
        out_shape = jax.ShapeDtypeStruct((chunks * CHUNK, LANES), jnp.float32)
    return pl.pallas_call(
        functools.partial(
            mix_kernel,
            [(row, start, length) for _, row, start, length in pieces],
            chunk_of,
            solve,
        ),
        in_specs=[anywhere] * len(pieces)
        + [pl.BlockSpec(memory_space=pltpu.VMEM)] * (1 if solve else 0)
        + [anywhere, pl.BlockSpec(memory_space=pltpu.VMEM)],
        out_specs=pl.BlockSpec(memory_space=pltpu.VMEM),
        out_shape=out_shape,
        scratch_shapes=[pltpu.VMEM((rows, LANES), jnp.float32)]
        + [pltpu.SMEM((near.shape[0], 1, CHUNK), jnp.int32)] * BUFFERS
        + [pltpu.SemaphoreType.DMA((BUFFERS,)), pltpu.SemaphoreType.DMA((len(pieces),))],
        compiler_params=pltpu.CompilerParams(vmem_limit_bytes=LIMIT),
        name="mix_solve" if solve else "mix",
    )(*[array for array, _, _, _ in pieces], *([solver] if solve else []), near, edges)


def to_neighbours(initial, last):
    count = lax.axis_size("blk")
    up = [(i, (i + 1) % count) for i in range(count)]
    down = [(j, i) for i, j in up]
    return lax.ppermute(last, "blk", up), lax.ppermute(initial, "blk", down)


def pick_rows(table, where):
    return jnp.take(table, where, axis=0)


def add_rows(values, where, count):
    start = jnp.zeros((count, values.shape[1]), jnp.float32)
    return start.at[where].add(values)


def shards(
    thermal_profiles,
    adjacent_positions,
    diffusion_link_factor,
    implicit_solver_matrix,
    lagged_surface_temp,
    flux_coefficient,
    flux_heating,
    ocean_cell_mask,
    atmosphere_slot_cells,
    ocean_slot_cells,
    forward_weight_blocks,
    backward_weight_blocks,
):
    blocks = lax.axis_size("blk")
    ocean_section = lax.axis_index("comp") == 1
    water_indicator = ocean_cell_mask.astype(jnp.float32)
    owner_state = thermal_profiles[0]
    level_stack, cell_count = owner_state.shape
    flux_count = flux_coefficient.shape[0]
    neighbours = adjacent_positions.shape[1]
    near = adjacent_positions.reshape(neighbours, 1, cell_count)
    edges = diffusion_link_factor.reshape(neighbours, 1, cell_count)
    solver = implicit_solver_matrix[0]

    before, after = to_neighbours(owner_state[:, :HALO], owner_state[:, cell_count - HALO :])

    atmosphere_flux = (
        flux_coefficient * (owner_state[level_stack - 1] - lagged_surface_temp)[None, :]
    )
    atm_slot_rows = atmosphere_slot_cells[0]
    slot_atm = atm_slot_rows.shape[1]
    payload = pick_rows(atmosphere_flux.T, atm_slot_rows.reshape(-1)).reshape(
        blocks, slot_atm * flux_count
    )
    padding = jnp.zeros_like(payload)
    outgoing = jnp.concatenate([padding, payload], axis=0)
    incoming = lax.all_to_all(outgoing, ("comp", "blk"), split_axis=0, concat_axis=0, tiled=True)
    arrived = incoming[:blocks]
    arrived_rows = arrived.reshape(blocks, slot_atm, flux_count)
    mapped = jnp.einsum("ajk,akf->ajf", forward_weight_blocks[0], arrived_rows, precision=HIGHEST)
    ocean_slot_row_list = ocean_slot_cells[0]
    slot_ocean = ocean_slot_row_list.shape[1]
    ocean_rows = add_rows(
        mapped.reshape(blocks * slot_ocean, flux_count), ocean_slot_row_list.reshape(-1), cell_count
    )
    ocean_flux = ocean_rows.T * water_indicator[None, :]
    driving_source = jnp.sum(flux_heating[:, None] * ocean_flux, axis=0)
    forcing = jnp.where(ocean_section, driving_source, jnp.zeros_like(driving_source))[None, :]

    forcing_before, forcing_after = to_neighbours(
        forcing[:, :HALO], forcing[:, cell_count - HALO :]
    )
    rows = to_rows(owner_state, forcing)
    rows_before = to_rows(before, forcing_before)
    rows_after = to_rows(after, forcing_after)

    halo_chunks = HALO // CHUNK
    chunks = cell_count // CHUNK
    middle = cell_count - 2 * HALO
    first_table = [
        (rows_before, 0, 0, HALO),
        (rows, 0, HALO, cell_count),
        (rows_after, 0, HALO + cell_count, HALO),
    ]
    rims = mix(
        first_table,
        near,
        edges,
        lambda i: jnp.where(i < halo_chunks, i, i + chunks - 2 * halo_chunks),
        2 * halo_chunks,
    )
    next_before, next_after = to_neighbours(rims[:HALO], rims[HALO:])
    inside = mix(first_table, near, edges, lambda i: i + halo_chunks, chunks - 2 * halo_chunks)
    second_table = [
        (next_before, 0, 0, HALO),
        (rims, 0, HALO, HALO),
        (inside, 0, 2 * HALO, middle),
        (rims, HALO, 2 * HALO + middle, HALO),
        (next_after, 0, HALO + cell_count, HALO),
    ]
    twice = jnp.dot(solver, solver, precision=HIGHEST)
    twice = jnp.pad(twice, ((0, 0), (0, LANES - level_stack)))
    current_state = mix(second_table, near, edges, lambda i: i, chunks, twice)

    sea_skin_warmth = current_state[0] * water_indicator
    return_payload = pick_rows(sea_skin_warmth, ocean_slot_row_list.reshape(-1)).reshape(
        blocks, slot_ocean
    )
    back_padding = jnp.zeros_like(return_payload)
    back_outgoing = jnp.concatenate([return_payload, back_padding], axis=0)
    back_incoming = lax.all_to_all(
        back_outgoing, ("comp", "blk"), split_axis=0, concat_axis=0, tiled=True
    )
    back_arrived = back_incoming[blocks:]
    remapped_return = jnp.einsum(
        "okj,oj->ok", backward_weight_blocks[0], back_arrived, precision=HIGHEST
    )
    atmosphere_surface_temp = add_rows(
        remapped_return.reshape(-1, 1), atm_slot_rows.reshape(-1), cell_count
    )[:, 0]
    flux_out = jnp.where(ocean_section, ocean_flux, atmosphere_flux)
    surface_output = jnp.where(ocean_section, sea_skin_warmth, atmosphere_surface_temp)
    return (current_state[None], flux_out[None], surface_output[None])


def solution(mesh):
    placed = (
        P("comp", None, "blk"),
        P("comp", None, "blk"),
        P("comp", None, "blk"),
        P("comp", None, None),
        P("blk"),
        P(None, "blk"),
        P(),
        P("blk"),
        P("blk", None, None),
        P("blk", None, None),
        P("blk", None, None, None),
        P("blk", None, None, None),
    )
    return jax.shard_map(
        shards,
        mesh=mesh,
        in_specs=placed,
        out_specs=(P("comp", None, "blk"), P("comp", None, "blk"), P("comp", "blk")),
        check_vma=False,
    )
```

```python
import functools

import jax
import jax.numpy as jnp
from jax import lax
from jax.experimental import pallas as pl
from jax.experimental.pallas import tpu as pltpu
from jax.sharding import PartitionSpec as P

HALO = 1024
CHUNK = 128
LANES = 128
WIDE = 256
SUB = 8
BUFFERS = 4
GROUP = 4
LIMIT = 56 * 2**20
HIGHEST = lax.Precision.HIGHEST


def split(value):
    high = value.astype(jnp.bfloat16)
    return high, (value - high.astype(jnp.float32)).astype(jnp.bfloat16)


def dot(a, b):
    return jnp.dot(a, b, preferred_element_type=jnp.float32)


def dot_nt(a, b):
    return lax.dot_general(a, b, (((1,), (1,)), ((), ())), preferred_element_type=jnp.float32)


def params():
    return pltpu.CompilerParams(vmem_limit_bytes=LIMIT)


def whole():
    return pl.BlockSpec(memory_space=pltpu.VMEM)


def scalars():
    return pl.BlockSpec(memory_space=pltpu.SMEM)


def anywhere():
    return pl.BlockSpec(memory_space=pl.ANY)


def lanes_from(row, lane):
    return jnp.take_along_axis(row, lane, axis=1)


def pick_lanes(count, tables, cells, parts=4):
    high, low = cells >> 7, cells & (LANES - 1)
    totals = []
    for part in range(parts):
        found = [jnp.zeros(cells.shape, jnp.float32) for _ in tables]
        for tile in range(part, count, parts):
            here = high == tile
            found = [
                jnp.where(here, lanes_from(table(tile), low), seen)
                for table, seen in zip(tables, found)
            ]
        totals.append(found)
    return [functools.reduce(lambda a, b: a + b, column) for column in zip(*totals)]


def pack_kernel(
    ocean_ref, coefficient_ref, own_ref, received_ref, lagged_ref, slot_ref, flux_ref, payload_ref
):
    fields, cells = coefficient_ref.shape
    for k in range(cells // LANES):
        cut = slice(k * LANES, (k + 1) * LANES)
        air = jnp.where(ocean_ref[0] == 1, received_ref[:, cut], own_ref[:, cut])
        flux_ref[:, cut] = coefficient_ref[:, cut] * (air - lagged_ref[:, cut])
    owners, slots = slot_ref.shape
    width = min(slots, LANES)
    pieces = slots // width

    def tile_of(base, k):
        return flux_ref[base : base + SUB, k * LANES : (k + 1) * LANES]

    tables = [functools.partial(tile_of, base) for base in range(0, fields, SUB)]

    def body(owner, carry):
        row = slot_ref[pl.ds(owner, 1), :]
        for piece in range(pieces):
            where = row[:, piece * width : (piece + 1) * width]
            if width < LANES:
                where = jnp.concatenate([where] * (LANES // width), axis=1)
            where = jnp.broadcast_to(where, (SUB, LANES))
            for n, found in enumerate(pick_lanes(cells // LANES, tables, where)):
                payload_ref[owner, n * SUB : (n + 1) * SUB, piece * width : (piece + 1) * width] = (
                    found[:, :width]
                )
        return carry

    lax.fori_loop(0, owners, body, 0, unroll=2)


def pack(ocean, coefficient, own, received, lagged, slots):
    fields, cells = coefficient.shape
    owners, count = slots.shape
    return pl.pallas_call(
        pack_kernel,
        in_specs=[scalars()] + [whole()] * 5,
        out_specs=[whole()] * 2,
        out_shape=[
            jax.ShapeDtypeStruct((fields, cells), jnp.float32),
            jax.ShapeDtypeStruct((owners, fields, count), jnp.float32),
        ],
        compiler_params=params(),
        name="pack",
    )(ocean, coefficient, own, received, lagged, slots)


def row_of(ref, k, width):
    tiles = width // LANES
    return jnp.concatenate([ref[k * tiles + t : k * tiles + t + 1, :] for t in range(tiles)], axis=1)


def one_of(low):
    shape = WIDE, low.shape[1]
    row = lax.broadcasted_iota(jnp.int32, shape, 0)
    return jnp.where(row == jnp.broadcast_to(low, shape), 1.0, 0.0).astype(jnp.bfloat16)


def fetch_blocks(weight_ref, held, sems):
    return lambda k: pltpu.make_async_copy(weight_ref.at[k], held.at[k], sems.at[k])


def forward_kernel(
    ocean_ref, heat_ref, weight_ref, arrived_ref, slot_ref, mask_ref, flux_ref, out_ref, source_ref,
    held, total, sems,
):
    owners, fields, _ = arrived_ref.shape
    slots = slot_ref.shape[1]
    highs = total.shape[0] // fields
    fetch = fetch_blocks(weight_ref, held, sems)
    for k in range(owners):
        fetch(k).start()
    total[...] = jnp.zeros_like(total)
    zero = jnp.zeros((fields, slots), jnp.bfloat16)

    def added(k):
        value_high, value_low = split(arrived_ref[k])
        weight_high, weight_low = split(held[k])
        both = dot_nt(jnp.concatenate([value_high, value_low], axis=0), weight_high)
        mapped = (both[fields:] + dot_nt(value_high, weight_low)) + both[:fields]
        parts = split(mapped)
        cell = slot_ref[pl.ds(k, 1), :]
        high = jnp.broadcast_to(cell >> 8, (fields, slots)).astype(jnp.float32)
        high = high.astype(jnp.bfloat16)
        spread = one_of(cell & (WIDE - 1))
        here = [high == jnp.bfloat16(h) for h in range(highs)]
        rows = [
            jnp.concatenate([jnp.where(here[h], part, zero) for h in range(highs)], axis=0)
            for part in parts
        ]
        return dot_nt(rows[1], spread) + dot_nt(rows[0], spread)

    def body(turn, carry):
        for k in range(GROUP):
            fetch(turn * GROUP + k).wait()
        parts = [added(turn * GROUP + k) for k in range(GROUP)]
        total[...] += functools.reduce(lambda a, b: a + b, parts)
        return carry

    lax.fori_loop(0, owners // GROUP, body, 0)
    ocean = ocean_ref[0]
    sub = lax.broadcasted_iota(jnp.int32, (fields, WIDE), 0)
    heat = jnp.zeros((fields, WIDE), jnp.float32)
    for f in range(fields):
        heat = jnp.where(sub == f, heat_ref[f], heat)
    for h in range(highs):
        cut = slice(h * WIDE, (h + 1) * WIDE)
        wet = row_of(mask_ref, h, WIDE).astype(jnp.float32)
        block = total[h * fields : (h + 1) * fields, :] * wet
        out_ref[:, cut] = jnp.where(ocean == 1, block, flux_ref[:, cut])
        source = jnp.sum(heat * block, axis=0, keepdims=True)
        source = jnp.where(ocean == 1, source, 0.0)
        for t in range(WIDE // LANES):
            at = h * (WIDE // LANES) + t
            source_ref[at : at + 1, :] = source[:, t * LANES : (t + 1) * LANES]


def forward(ocean, heating, weights, arrived, slots, mask, flux):
    owners, fields, _ = arrived.shape
    cells = flux.shape[1]
    return pl.pallas_call(
        forward_kernel,
        in_specs=[scalars()] * 2 + [anywhere()] + [whole()] * 4,
        out_specs=[whole()] * 2,
        out_shape=[
            jax.ShapeDtypeStruct((fields, cells), jnp.float32),
            jax.ShapeDtypeStruct((cells // LANES, LANES), jnp.float32),
        ],
        scratch_shapes=[
            pltpu.VMEM(weights.shape, jnp.float32),
            pltpu.VMEM((cells // WIDE * fields, WIDE), jnp.float32),
            pltpu.SemaphoreType.DMA((owners,)),
        ],
        compiler_params=params(),
        name="forward",
    )(ocean, heating, weights, arrived, slots, mask, flux)


def mix_source_kernel(before_ref, own_ref, after_ref, near_ref, edge_ref, _, out_ref):
    tiles = own_ref.shape[0]
    rim = before_ref.shape[0]
    neighbours = near_ref.shape[0]

    def tile_of(k):
        if k < rim:
            row = before_ref[k : k + 1, :]
        elif k < rim + tiles:
            row = own_ref[k - rim : k - rim + 1, :]
        else:
            row = after_ref[k - rim - tiles : k - rim - tiles + 1, :]
        return jnp.broadcast_to(row, (SUB, LANES))

    def body(group, carry):
        at = pl.ds(pl.multiple_of(group * SUB, SUB), SUB)
        keep = jnp.ones((SUB, LANES), jnp.float32)
        total = jnp.zeros((SUB, LANES), jnp.float32)
        for j in range(neighbours):
            edge = edge_ref[j, at, :]
            (found,) = pick_lanes(tiles + 2 * rim, [tile_of], near_ref[j, at, :])
            total = total + edge * found
            keep = keep - edge
        out_ref[at, :] = total + keep * own_ref[at, :]
        return carry

    lax.fori_loop(0, tiles // SUB, body, 0)


def mix_source(before, own, after, near, edges, wait):
    shape = near.shape[0], own.shape[0], LANES
    return pl.pallas_call(
        mix_source_kernel,
        in_specs=[whole()] * 5 + [anywhere()],
        out_specs=whole(),
        out_shape=jax.ShapeDtypeStruct(own.shape, jnp.float32),
        compiler_params=params(),
        name="mix_source",
    )(before, own, after, near.reshape(shape), edges.reshape(shape), wait)


def backward_kernel(
    ocean_ref, weight_ref, arrived_ref, slot_ref, surface_ref, out_ref, held, total, sems
):
    owners, slots = slot_ref.shape
    highs = total.shape[0]
    fetch = fetch_blocks(weight_ref, held, sems)
    for k in range(owners):
        fetch(k).start()
    total[...] = jnp.zeros_like(total)

    def added(k):
        weight_high, weight_low = split(held[k])
        value = arrived_ref[pl.ds(owners + k, 1), :]
        value = jnp.broadcast_to(value, (2 * SUB, value.shape[1]))
        value_high, value_low = split(value)
        mapped = (dot_nt(value_low, weight_high) + dot_nt(value_high, weight_low)) + dot_nt(
            value_high, weight_high
        )
        mapped = jnp.broadcast_to(mapped[:1], (highs, slots))
        cell = slot_ref[pl.ds(k, 1), :]
        high = jnp.broadcast_to(cell >> 8, (highs, slots))
        spread = one_of(cell & (WIDE - 1))
        here = lax.broadcasted_iota(jnp.int32, (highs, slots), 0) == high
        part_high, part_low = split(jnp.where(here, mapped, 0.0))
        return dot_nt(part_low, spread) + dot_nt(part_high, spread)

    def body(turn, carry):
        for k in range(GROUP):
            fetch(turn * GROUP + k).wait()
        parts = [added(turn * GROUP + k) for k in range(GROUP)]
        total[...] += functools.reduce(lambda a, b: a + b, parts)
        return carry

    lax.fori_loop(0, owners // GROUP, body, 0)
    for h in range(highs):
        row = jnp.where(ocean_ref[0] == 1, row_of(surface_ref, h, WIDE), total[h : h + 1, :])
        out_ref[:, h * WIDE : (h + 1) * WIDE] = row


def backward(ocean, weights, arrived, slots, surface):
    owners, _ = slots.shape
    cells = surface.shape[0] * LANES
    return pl.pallas_call(
        backward_kernel,
        in_specs=[scalars(), anywhere()] + [whole()] * 3,
        out_specs=whole(),
        out_shape=jax.ShapeDtypeStruct((1, cells), jnp.float32),
        scratch_shapes=[
            pltpu.VMEM(weights.shape, jnp.float32),
            pltpu.VMEM((cells // WIDE, WIDE), jnp.float32),
            pltpu.SemaphoreType.DMA((owners,)),
        ],
        compiler_params=params(),
        name="backward",
    )(ocean, weights, arrived, slots, surface)


def mixer(near_ref, edge_ref, table, factors, slots, near_sems, chunk_of, chunks):
    neighbours = near_ref.shape[0]

    def fetch(i, slot):
        start = pl.multiple_of(chunk_of(i) * CHUNK, CHUNK)
        return pltpu.make_async_copy(
            near_ref.at[:, :, pl.ds(start, CHUNK)], slots[slot], near_sems.at[slot]
        )

    def begin():
        for slot in range(BUFFERS - 1):
            fetch(slot, slot).start()

    def set_factors(i, half):
        cell = pl.multiple_of(chunk_of(i) * CHUNK, CHUNK)
        edges = [edge_ref[j, :, pl.ds(cell, CHUNK)] for j in range(neighbours)]
        keep = 1.0 - functools.reduce(lambda a, b: a + b, edges)
        rest = jnp.zeros((SUB - neighbours - 1, CHUNK), jnp.float32)
        factors[half] = jnp.concatenate(edges + [keep, rest], axis=0).T

    def run(ahead, emit):
        set_factors(0, 0)
        sub = lax.broadcasted_iota(jnp.int32, (SUB, LANES), 0)
        masks = [sub == s for s in range(SUB)]

        def body(turn, carry):
            for slot in range(BUFFERS):
                i = turn * BUFFERS + slot
                half = slot % 2
                fetch(i, slot).wait()

                @pl.when(i + BUFFERS - 1 < chunks)
                def _():
                    fetch(i + BUFFERS - 1, (slot + BUFFERS - 1) % BUFFERS).start()

                ahead(turn, slot, i)
                set_factors(jnp.minimum(i + 1, chunks - 1), 1 - half)
                cell = pl.multiple_of(chunk_of(i) * CHUNK, CHUNK)
                for g in range(CHUNK // SUB):
                    own = table[pl.ds(pl.multiple_of(HALO + cell + g * SUB, SUB), SUB), :]
                    part = factors[half, g * SUB : (g + 1) * SUB, :]
                    total = own * jnp.broadcast_to(
                        part[:, neighbours : neighbours + 1], (SUB, LANES)
                    )
                    for j in range(neighbours):
                        picked = None
                        for s in range(SUB):
                            where = slots[slot][j, 0, g * SUB + s]
                            row = jnp.broadcast_to(table[pl.ds(where, 1), :], (SUB, LANES))
                            picked = row if s == 0 else jnp.where(masks[s], row, picked)
                        total = total + jnp.broadcast_to(part[:, j : j + 1], (SUB, LANES)) * picked
                    emit(i, half, g * SUB, total)
            return carry

        lax.fori_loop(0, chunks // BUFFERS, body, 0)

    return begin, run


def run_rows(run, chunks, rows, out_ref, out_sems):
    length = BUFFERS * CHUNK
    turns = chunks // BUFFERS

    def copy(turn):
        at = pl.ds(pl.multiple_of(turn * length, length), length)
        return pltpu.make_async_copy(rows.at[at], out_ref.at[at], out_sems.at[turn])

    def ahead(turn, slot, i):
        if slot == 1:

            @pl.when(turn > 0)
            def _():
                copy(turn - 1).start()

    def emit(i, half, start, total):
        rows[pl.ds(pl.multiple_of(i * CHUNK + start, SUB), SUB), :] = total

    run(ahead, emit)
    copy(turns - 1).start()
    for turn in range(turns):
        copy(turn).wait()


def run_solve(run, chunks, solver_ref, mixed, levels, out_ref, out_sems):
    length = BUFFERS * CHUNK
    turns = chunks // BUFFERS

    def copy(turn):
        at = pl.ds(pl.multiple_of(turn * length, length), length)
        return pltpu.make_async_copy(levels.at[:, at], out_ref.at[:, at], out_sems.at[turn])

    def solve(i, half):
        high, low = split(mixed[half])
        solver_high, solver_low = split(solver_ref[...])
        levels[:, pl.ds(pl.multiple_of(i * CHUNK, CHUNK), CHUNK)] = (
            dot_nt(solver_high, low) + dot_nt(solver_low, high)
        ) + dot_nt(solver_high, high)

    def ahead(turn, slot, i):
        if slot == 1:

            @pl.when(turn > 0)
            def _():
                copy(turn - 1).start()

        solve(jnp.maximum(i - 1, 0), 1 - slot % 2)

    def emit(i, half, start, total):
        mixed[half, start : start + SUB, :] = total

    mixed[...] = jnp.zeros_like(mixed)
    run(ahead, emit)
    solve(chunks - 1, (chunks - 1) % 2)
    copy(turns - 1).start()
    for turn in range(turns):
        copy(turn).wait()


def mixer_scratch(rows, neighbours, turns):
    return [
        pltpu.VMEM((rows, LANES), jnp.float32),
        pltpu.VMEM((2, CHUNK, SUB), jnp.float32),
        *[pltpu.SMEM((neighbours, 1, CHUNK), jnp.int32)] * BUFFERS,
        pltpu.SemaphoreType.DMA((BUFFERS,)),
        pltpu.SemaphoreType.DMA((turns,)),
    ]


def rims_kernel(chunk_of, chunks, *refs):
    state_ref, before_ref, after_ref, near_ref, edge_ref, *refs = refs
    out_ref, table_ref, *refs = refs
    table, factors, *slots, near_sems, out_sems, field, rows, load_sems, table_sem = refs
    levels, cells = state_ref.shape
    places = [(before_ref, 0, HALO), (state_ref, HALO, cells), (after_ref, HALO + cells, HALO)]
    loads = [
        pltpu.make_async_copy(ref, field.at[:, pl.ds(start, length)], load_sems.at[k])
        for k, (ref, start, length) in enumerate(places)
    ]
    begin, run = mixer(near_ref, edge_ref, table, factors, slots, near_sems, chunk_of, chunks)
    for load in loads:
        load.start()
    begin()
    for load in loads:
        load.wait()
    rest = jnp.zeros((LANES - levels, LANES), jnp.float32)

    def turn_tiles(k, carry):
        width = SUB * LANES
        start = pl.multiple_of(k * width, width)
        block = field[:, pl.ds(start, width)]
        for t in range(SUB):
            tile = jnp.concatenate([block[:, t * LANES : (t + 1) * LANES], rest], axis=0)
            table[pl.ds(pl.multiple_of(start + t * LANES, LANES), LANES), :] = tile.T
        return carry

    lax.fori_loop(0, table.shape[0] // (SUB * LANES), turn_tiles, 0)
    save = pltpu.make_async_copy(table, table_ref, table_sem)
    save.start()
    run_rows(run, chunks, rows, out_ref, out_sems)
    save.wait()


def mix_rims(state, before, after, near, edges, chunk_of, chunks):
    levels, cells = state.shape
    extended = cells + 2 * HALO
    return pl.pallas_call(
        functools.partial(rims_kernel, chunk_of, chunks),
        in_specs=[anywhere()] * 4 + [whole()],
        out_specs=[anywhere(), anywhere()],
        out_shape=[
            jax.ShapeDtypeStruct((chunks * CHUNK, LANES), jnp.float32),
            jax.ShapeDtypeStruct((extended, LANES), jnp.float32),
        ],
        scratch_shapes=mixer_scratch(extended, near.shape[0], chunks // BUFFERS)
        + [
            pltpu.VMEM((levels, extended), jnp.float32),
            pltpu.VMEM((chunks * CHUNK, LANES), jnp.float32),
            pltpu.SemaphoreType.DMA((3,)),
            pltpu.SemaphoreType.DMA,
        ],
        compiler_params=params(),
        name="mix_rims",
    )(state, before, after, near, edges)


def inside_kernel(chunk_of, chunks, *refs):
    table_ref, near_ref, edge_ref, _, out_ref, *refs = refs
    table, factors, *slots, near_sems, out_sems, rows, table_sem = refs
    load = pltpu.make_async_copy(table_ref, table, table_sem)
    load.start()
    begin, run = mixer(near_ref, edge_ref, table, factors, slots, near_sems, chunk_of, chunks)
    begin()
    load.wait()
    run_rows(run, chunks, rows, out_ref, out_sems)


def mix_inside(table, near, edges, wait, chunk_of, chunks):
    return pl.pallas_call(
        functools.partial(inside_kernel, chunk_of, chunks),
        in_specs=[anywhere()] * 2 + [whole(), anywhere()],
        out_specs=anywhere(),
        out_shape=jax.ShapeDtypeStruct((chunks * CHUNK, LANES), jnp.float32),
        scratch_shapes=mixer_scratch(table.shape[0], near.shape[0], chunks // BUFFERS)
        + [pltpu.VMEM((chunks * CHUNK, LANES), jnp.float32), pltpu.SemaphoreType.DMA],
        compiler_params=params(),
        name="mix_inside",
    )(table, near, edges, wait)


def solve_kernel(pieces, *refs):
    piece_refs, refs = refs[: len(pieces)], refs[len(pieces) :]
    solver_ref, before_ref, own_ref, after_ref, mask_ref, slot_ref, near_ref, edge_ref, *refs = refs
    out_ref, surface_ref, payload_ref, *refs = refs
    table, factors, *slots, near_sems, out_sems, mixed, levels, piece_sems = refs
    chunks = out_ref.shape[1] // CHUNK
    tiles = own_ref.shape[0]
    loads = [
        pltpu.make_async_copy(
            ref.at[pl.ds(row, length)], table.at[pl.ds(start, length)], piece_sems.at[k]
        )
        for k, (ref, (row, start, length)) in enumerate(zip(piece_refs, pieces))
    ]
    for load in loads:
        load.start()
    begin, run = mixer(near_ref, edge_ref, table, factors, slots, near_sems, lambda i: i, chunks)
    begin()
    for load in loads:
        load.wait()
    lane = lax.broadcasted_iota(jnp.int32, (LANES, LANES), 1)

    def add_source(source_ref, first, start):
        columns = source_ref[pl.ds(first, SUB), :].T
        for t in range(SUB):
            at = pl.ds(pl.multiple_of(start + t * LANES, LANES), LANES)
            column = jnp.broadcast_to(columns[:, t : t + 1], (LANES, LANES))
            table[at, :] = table[at, :] + jnp.where(lane == 0, column, 0.0)

    def add_own(k, carry):
        first = pl.multiple_of(k * SUB, SUB)
        add_source(own_ref, first, HALO + first * LANES)
        return carry

    add_source(before_ref, 0, 0)
    lax.fori_loop(0, tiles // SUB, add_own, 0)
    add_source(after_ref, 0, HALO + tiles * LANES)
    run_solve(run, chunks, solver_ref, mixed, levels, out_ref, out_sems)

    for k in range(tiles):
        wet = mask_ref[k : k + 1, :].astype(jnp.float32)
        surface_ref[k : k + 1, :] = levels[:1, k * LANES : (k + 1) * LANES] * wet
    owners, slots = slot_ref.shape
    payload_ref[owners:, :] = jnp.zeros((owners, slots), jnp.float32)

    def surface_tile(k):
        return jnp.broadcast_to(surface_ref[k : k + 1, :], (SUB, LANES))

    def pick(group, carry):
        at = pl.ds(pl.multiple_of(group * SUB, SUB), SUB)
        for k in range(slots // LANES):
            cut = slice(k * LANES, (k + 1) * LANES)
            (found,) = pick_lanes(tiles, [surface_tile], slot_ref[at, cut])
            payload_ref[at, cut] = found
        return carry

    lax.fori_loop(0, owners // SUB, pick, 0)


def mix_solve(pieces, solver, before, own, after, mask, slots, near, edges):
    rows = sum(length for _, _, _, length in pieces)
    cells = own.shape[0] * LANES
    owners, count = slots.shape
    return pl.pallas_call(
        functools.partial(solve_kernel, [(row, start, length) for _, row, start, length in pieces]),
        in_specs=[anywhere()] * len(pieces)
        + [whole()] * 6
        + [anywhere(), whole()],
        out_specs=[anywhere(), whole(), whole()],
        out_shape=[
            jax.ShapeDtypeStruct((solver.shape[0], cells), jnp.float32),
            jax.ShapeDtypeStruct(own.shape, jnp.float32),
            jax.ShapeDtypeStruct((2 * owners, count), jnp.float32),
        ],
        scratch_shapes=mixer_scratch(rows, near.shape[0], cells // CHUNK // BUFFERS)
        + [
            pltpu.VMEM((2, CHUNK, LANES), jnp.float32),
            pltpu.VMEM((solver.shape[0], cells), jnp.float32),
            pltpu.SemaphoreType.DMA((len(pieces),)),
        ],
        compiler_params=params(),
        name="mix_solve",
    )(*[array for array, _, _, _ in pieces], solver, before, own, after, mask, slots, near, edges)


def to_neighbours(initial, last):
    count = lax.axis_size("blk")
    up = [(i, (i + 1) % count) for i in range(count)]
    down = [(j, i) for i, j in up]
    return lax.ppermute(last, "blk", up), lax.ppermute(initial, "blk", down)


def exchange(array, axes):
    return lax.all_to_all(array, axes, split_axis=0, concat_axis=0, tiled=True)


def shards(
    thermal_profiles,
    adjacent_positions,
    diffusion_link_factor,
    implicit_solver_matrix,
    lagged_surface_temp,
    flux_coefficient,
    flux_heating,
    ocean_cell_mask,
    atmosphere_slot_cells,
    ocean_slot_cells,
    forward_weight_blocks,
    backward_weight_blocks,
):
    ocean = lax.axis_index("comp").astype(jnp.int32).reshape(1)
    state = thermal_profiles[0]
    levels, cells = state.shape
    neighbours = adjacent_positions.shape[1]
    near = adjacent_positions.reshape(neighbours, 1, cells)
    edges = diffusion_link_factor.reshape(neighbours, 1, cells)
    mask = ocean_cell_mask.reshape(cells // LANES, LANES)
    atmosphere_slots = atmosphere_slot_cells[0]
    ocean_slots = ocean_slot_cells[0]
    solver = implicit_solver_matrix[0]
    twice = jnp.dot(solver, solver, precision=HIGHEST)
    twice = jnp.pad(twice, ((0, 0), (0, LANES - levels)))

    lowest = state[levels - 1 :]
    flux, payload = pack(
        ocean,
        flux_coefficient,
        lowest,
        lax.ppermute(lowest, "comp", [(0, 1)]),
        lagged_surface_temp.reshape(1, cells),
        atmosphere_slots,
    )
    arrived = exchange(payload, "blk")

    before, after = to_neighbours(state[:, :HALO], state[:, cells - HALO :])
    rim = HALO // CHUNK
    chunks = cells // CHUNK
    half = (chunks - 2 * rim) // 2
    rims, table = mix_rims(
        state,
        before,
        after,
        near,
        edges,
        lambda i: jnp.where(i < rim, i, i + chunks - 2 * rim),
        2 * rim,
    )
    next_before, next_after = to_neighbours(rims[:HALO], rims[HALO:])

    flux_out, source = forward(
        ocean,
        flux_heating,
        forward_weight_blocks[0],
        arrived,
        ocean_slots,
        mask,
        flux,
    )
    rim_rows = HALO // LANES
    source_before, source_after = to_neighbours(source[:rim_rows], source[-rim_rows:])
    low = mix_inside(table, near, edges, source, lambda i: i + rim, half)
    mixed = mix_source(source_before, source, source_after, near, edges, low)
    mixed_before, mixed_after = to_neighbours(mixed[:rim_rows], mixed[-rim_rows:])
    high = mix_inside(table, near, edges, mixed, lambda i: i + rim + half, half)

    middle = half * CHUNK
    result, surface, back_payload = mix_solve(
        [
            (next_before, 0, 0, HALO),
            (rims, 0, HALO, HALO),
            (low, 0, 2 * HALO, middle),
            (high, 0, 2 * HALO + middle, middle),
            (rims, HALO, 2 * HALO + 2 * middle, HALO),
            (next_after, 0, HALO + cells, HALO),
        ],
        twice,
        mixed_before,
        mixed,
        mixed_after,
        mask,
        ocean_slots,
        near,
        edges,
    )
    warmth = backward(
        ocean,
        backward_weight_blocks[0],
        exchange(back_payload, ("comp", "blk")),
        atmosphere_slots,
        surface,
    )
    return (result[None], flux_out[None], warmth)


def solution(mesh):
    placed = (
        P("comp", None, "blk"),
        P("comp", None, "blk"),
        P("comp", None, "blk"),
        P("comp", None, None),
        P("blk"),
        P(None, "blk"),
        P(),
        P("blk"),
        P("blk", None, None),
        P("blk", None, None),
        P("blk", None, None, None),
        P("blk", None, None, None),
    )
    return jax.shard_map(
        shards,
        mesh=mesh,
        in_specs=placed,
        out_specs=(P("comp", None, "blk"), P("comp", None, "blk"), P("comp", "blk")),
        check_vma=False,
    )
```

```python
import functools

import jax
import jax.numpy as jnp
from jax import lax
from jax.experimental import pallas as pl
from jax.experimental.pallas import tpu as pltpu
from jax.sharding import PartitionSpec as P

HALO = 1024
CHUNK = 256
LANES = 128
WIDE = 256
SUB = 8
BUFFERS = 4
GROUP = 4
HIGHEST = lax.Precision.HIGHEST


def split(value):
    high = value.astype(jnp.bfloat16)
    return high, (value - high.astype(jnp.float32)).astype(jnp.bfloat16)


def dot(a, b):
    return jnp.dot(a, b, preferred_element_type=jnp.float32)


def dot_nt(a, b):
    return lax.dot_general(a, b, (((1,), (1,)), ((), ())), preferred_element_type=jnp.float32)


def params(mebibytes=8):
    return pltpu.CompilerParams(vmem_limit_bytes=mebibytes * 2**20)


def whole():
    return pl.BlockSpec(memory_space=pltpu.VMEM)


def scalars():
    return pl.BlockSpec(memory_space=pltpu.SMEM)


def anywhere():
    return pl.BlockSpec(memory_space=pl.ANY)


def outside():
    return pl.BlockSpec(memory_space=pltpu.HBM)


def far(array):
    return pltpu.with_memory_space_constraint(array, pltpu.HBM)


def near_by(array):
    return pltpu.with_memory_space_constraint(array, pltpu.VMEM)


def lanes_from(row, lane):
    return jnp.take_along_axis(row, lane, axis=1)


def pick_lanes(count, tables, cells, parts=4):
    high, low = cells >> 7, cells & (LANES - 1)
    totals = []
    for part in range(parts):
        found = [jnp.zeros(cells.shape, jnp.float32) for _ in tables]
        for tile in range(part, count, parts):
            here = high == tile
            found = [
                jnp.where(here, lanes_from(table(tile), low), seen)
                for table, seen in zip(tables, found)
            ]
        totals.append(found)
    return [functools.reduce(lambda a, b: a + b, column) for column in zip(*totals)]


def pack_kernel(
    ocean_ref, coefficient_ref, own_ref, received_ref, lagged_ref, slot_ref, flux_ref, payload_ref
):
    fields, cells = coefficient_ref.shape
    for k in range(cells // LANES):
        cut = slice(k * LANES, (k + 1) * LANES)
        air = jnp.where(ocean_ref[0] == 1, received_ref[:, cut], own_ref[:, cut])
        flux_ref[:, cut] = coefficient_ref[:, cut] * (air - lagged_ref[:, cut])
    owners, slots = slot_ref.shape
    width = min(slots, LANES)
    pieces = slots // width

    def tile_of(base, k):
        return flux_ref[base : base + SUB, k * LANES : (k + 1) * LANES]

    tables = [functools.partial(tile_of, base) for base in range(0, fields, SUB)]

    def body(owner, carry):
        row = slot_ref[pl.ds(owner, 1), :]
        for piece in range(pieces):
            where = row[:, piece * width : (piece + 1) * width]
            if width < LANES:
                where = jnp.concatenate([where] * (LANES // width), axis=1)
            where = jnp.broadcast_to(where, (SUB, LANES))
            for n, found in enumerate(pick_lanes(cells // LANES, tables, where)):
                payload_ref[owner, n * SUB : (n + 1) * SUB, piece * width : (piece + 1) * width] = (
                    found[:, :width]
                )
        return carry

    lax.fori_loop(0, owners, body, 0, unroll=2)


def pack(ocean, coefficient, own, received, lagged, slots):
    fields, cells = coefficient.shape
    owners, count = slots.shape
    return pl.pallas_call(
        pack_kernel,
        in_specs=[scalars()] + [whole()] * 5,
        out_specs=[whole()] * 2,
        out_shape=[
            pltpu.VMEM((fields, cells), jnp.float32),
            jax.ShapeDtypeStruct((owners, fields, count), jnp.float32),
        ],
        compiler_params=params(),
        name="pack",
    )(ocean, coefficient, own, received, lagged, slots)


def row_of(ref, k, width):
    tiles = width // LANES
    return jnp.concatenate([ref[k * tiles + t : k * tiles + t + 1, :] for t in range(tiles)], axis=1)


def one_of(low):
    shape = WIDE, low.shape[1]
    row = lax.broadcasted_iota(jnp.int32, shape, 0)
    return jnp.where(row == jnp.broadcast_to(low, shape), 1.0, 0.0).astype(jnp.bfloat16)


def forward_kernel(
    ocean_ref, heat_ref, weight_ref, arrived_ref, slot_ref, mask_ref, flux_ref, out_ref, source_ref,
    held, total, sems,
):
    owners, fields, _ = arrived_ref.shape
    slots = slot_ref.shape[1]
    highs = total.shape[0] // fields

    def fetch(k):
        return pltpu.make_async_copy(weight_ref.at[k], held.at[k], sems.at[k])

    for k in range(owners):
        fetch(k).start()
    total[...] = jnp.zeros_like(total)
    zero = jnp.zeros((fields, slots), jnp.bfloat16)

    def added(k):
        value_high, value_low = split(arrived_ref[k])
        weight_high, weight_low = split(held[k])
        both = dot_nt(jnp.concatenate([value_high, value_low], axis=0), weight_high)
        mapped = (both[fields:] + dot_nt(value_high, weight_low)) + both[:fields]
        parts = split(mapped)
        cell = slot_ref[pl.ds(k, 1), :]
        high = jnp.broadcast_to(cell >> 8, (fields, slots)).astype(jnp.float32)
        high = high.astype(jnp.bfloat16)
        spread = one_of(cell & (WIDE - 1))
        here = [high == jnp.bfloat16(h) for h in range(highs)]
        rows = [
            jnp.concatenate([jnp.where(here[h], part, zero) for h in range(highs)], axis=0)
            for part in parts
        ]
        return dot_nt(rows[1], spread) + dot_nt(rows[0], spread)

    def body(turn, carry):
        for k in range(GROUP):
            fetch(turn * GROUP + k).wait()
        parts = [added(turn * GROUP + k) for k in range(GROUP)]
        total[...] += functools.reduce(lambda a, b: a + b, parts)
        return carry

    lax.fori_loop(0, owners // GROUP, body, 0)
    ocean = ocean_ref[0]
    sub = lax.broadcasted_iota(jnp.int32, (fields, WIDE), 0)
    heat = jnp.zeros((fields, WIDE), jnp.float32)
    for f in range(fields):
        heat = jnp.where(sub == f, heat_ref[f], heat)
    for h in range(highs):
        cut = slice(h * WIDE, (h + 1) * WIDE)
        wet = row_of(mask_ref, h, WIDE).astype(jnp.float32)
        block = total[h * fields : (h + 1) * fields, :] * wet
        out_ref[:, cut] = jnp.where(ocean == 1, block, flux_ref[:, cut])
        source = jnp.sum(heat * block, axis=0, keepdims=True)
        source = jnp.where(ocean == 1, source, 0.0)
        for t in range(WIDE // LANES):
            at = h * (WIDE // LANES) + t
            source_ref[at : at + 1, :] = source[:, t * LANES : (t + 1) * LANES]


def forward(ocean, heating, weights, arrived, slots, mask, flux):
    owners, fields, _ = arrived.shape
    cells = flux.shape[1]
    return pl.pallas_call(
        forward_kernel,
        in_specs=[scalars()] * 2 + [outside()] + [whole()] * 4,
        out_specs=[whole()] * 2,
        out_shape=[
            jax.ShapeDtypeStruct((fields, cells), jnp.float32),
            jax.ShapeDtypeStruct((cells // LANES, LANES), jnp.float32),
        ],
        scratch_shapes=[
            pltpu.VMEM(weights.shape, jnp.float32),
            pltpu.VMEM((cells // WIDE * fields, WIDE), jnp.float32),
            pltpu.SemaphoreType.DMA((owners,)),
        ],
        compiler_params=params(24),
        name="forward",
    )(ocean, heating, weights, arrived, slots, mask, flux)


def mix_source_kernel(before_ref, own_ref, after_ref, near_ref, edge_ref, _, out_ref):
    tiles = own_ref.shape[0]
    rim = before_ref.shape[0]
    neighbours = near_ref.shape[0]

    def tile_of(k):
        if k < rim:
            row = before_ref[k : k + 1, :]
        elif k < rim + tiles:
            row = own_ref[k - rim : k - rim + 1, :]
        else:
            row = after_ref[k - rim - tiles : k - rim - tiles + 1, :]
        return jnp.broadcast_to(row, (SUB, LANES))

    def body(group, carry):
        at = pl.ds(pl.multiple_of(group * SUB, SUB), SUB)
        keep = jnp.ones((SUB, LANES), jnp.float32)
        total = jnp.zeros((SUB, LANES), jnp.float32)
        for j in range(neighbours):
            edge = edge_ref[j, at, :]
            (found,) = pick_lanes(tiles + 2 * rim, [tile_of], near_ref[j, at, :])
            total = total + edge * found
            keep = keep - edge
        out_ref[at, :] = total + keep * own_ref[at, :]
        return carry

    lax.fori_loop(0, tiles // SUB, body, 0)


def mix_source(before, own, after, near, edges, wait):
    return pl.pallas_call(
        mix_source_kernel,
        in_specs=[whole()] * 5 + [anywhere()],
        out_specs=whole(),
        out_shape=jax.ShapeDtypeStruct(own.shape, jnp.float32),
        compiler_params=params(),
        name="mix_source",
    )(before, own, after, near, edges, wait)


def backward_kernel(
    ocean_ref, weight_ref, arrived_ref, slot_ref, surface_ref, out_ref, total
):
    owners, slots = slot_ref.shape
    highs = total.shape[0]
    total[...] = jnp.zeros_like(total)

    def added(k):
        weight_high, weight_low = split(weight_ref[k])
        value = arrived_ref[pl.ds(owners + k, 1), :]
        value = jnp.broadcast_to(value, (2 * SUB, value.shape[1]))
        value_high, value_low = split(value)
        mapped = (dot_nt(value_low, weight_high) + dot_nt(value_high, weight_low)) + dot_nt(
            value_high, weight_high
        )
        mapped = jnp.broadcast_to(mapped[:1], (highs, slots))
        cell = slot_ref[pl.ds(k, 1), :]
        high = jnp.broadcast_to(cell >> 8, (highs, slots))
        spread = one_of(cell & (WIDE - 1))
        here = lax.broadcasted_iota(jnp.int32, (highs, slots), 0) == high
        part_high, part_low = split(jnp.where(here, mapped, 0.0))
        return dot_nt(part_low, spread) + dot_nt(part_high, spread)

    def body(turn, carry):
        parts = [added(turn * GROUP + k) for k in range(GROUP)]
        total[...] += functools.reduce(lambda a, b: a + b, parts)
        return carry

    lax.fori_loop(0, owners // GROUP, body, 0)
    for h in range(highs):
        row = jnp.where(ocean_ref[0] == 1, row_of(surface_ref, h, WIDE), total[h : h + 1, :])
        out_ref[:, h * WIDE : (h + 1) * WIDE] = row


def backward(ocean, weights, arrived, slots, surface):
    owners, _ = slots.shape
    cells = surface.shape[0] * LANES
    return pl.pallas_call(
        backward_kernel,
        in_specs=[scalars()] + [whole()] * 4,
        out_specs=whole(),
        out_shape=jax.ShapeDtypeStruct((1, cells), jnp.float32),
        scratch_shapes=[
            pltpu.VMEM((cells // WIDE, WIDE), jnp.float32),
        ],
        compiler_params=params(),
        name="backward",
    )(ocean, weights, arrived, slots, surface)


def mixer(near_ref, edge_ref, table, factors, slots, near_sems, chunk_of, chunks):
    neighbours = near_ref.shape[0]

    def fetch(i, slot):
        start = pl.multiple_of(chunk_of(i) * CHUNK, CHUNK)
        return pltpu.make_async_copy(
            near_ref.at[:, :, pl.ds(start, CHUNK)], slots[slot], near_sems.at[slot]
        )

    def begin():
        for slot in range(BUFFERS - 1):
            fetch(slot, slot).start()

    def set_factors(i, half):
        tiles = CHUNK // LANES
        edges = [
            jnp.concatenate(
                [edge_ref[j, pl.ds(chunk_of(i) * tiles + t, 1), :] for t in range(tiles)], axis=1
            )
            for j in range(neighbours)
        ]
        keep = 1.0 - functools.reduce(lambda a, b: a + b, edges)
        rest = jnp.zeros((SUB - neighbours - 1, CHUNK), jnp.float32)
        factors[half] = jnp.concatenate(edges + [keep, rest], axis=0).T

    def run(ahead, emit):
        set_factors(0, 0)
        sub = lax.broadcasted_iota(jnp.int32, (SUB, LANES), 0)
        masks = [sub == s for s in range(SUB)]

        def body(turn, carry):
            for slot in range(BUFFERS):
                i = turn * BUFFERS + slot
                half = slot % 2
                fetch(i, slot).wait()

                @pl.when(i + BUFFERS - 1 < chunks)
                def _():
                    fetch(i + BUFFERS - 1, (slot + BUFFERS - 1) % BUFFERS).start()

                ahead(turn, slot, i)
                set_factors(jnp.minimum(i + 1, chunks - 1), 1 - half)
                cell = pl.multiple_of(chunk_of(i) * CHUNK, CHUNK)
                for g in range(CHUNK // SUB):
                    own = table[pl.ds(pl.multiple_of(HALO + cell + g * SUB, SUB), SUB), :]
                    part = factors[half, g * SUB : (g + 1) * SUB, :]
                    total = own * jnp.broadcast_to(
                        part[:, neighbours : neighbours + 1], (SUB, LANES)
                    )
                    for j in range(neighbours):
                        picked = None
                        for s in range(SUB):
                            where = slots[slot][j, 0, g * SUB + s]
                            row = jnp.broadcast_to(table[pl.ds(where, 1), :], (SUB, LANES))
                            picked = row if s == 0 else jnp.where(masks[s], row, picked)
                        total = total + jnp.broadcast_to(part[:, j : j + 1], (SUB, LANES)) * picked
                    emit(i, half, g * SUB, total)
            return carry

        lax.fori_loop(0, chunks // BUFFERS, body, 0)

    return begin, run


def run_solve(run, chunks, solver_ref, mixed, levels, out_ref, out_sems):
    length = BUFFERS * CHUNK
    turns = chunks // BUFFERS

    def copy(turn):
        at = pl.ds(pl.multiple_of(turn * length, length), length)
        return pltpu.make_async_copy(levels.at[:, at], out_ref.at[:, at], out_sems.at[turn])

    def solve(i, half):
        high, low = split(mixed[half])
        solver_high, solver_low = split(solver_ref[...])
        levels[:, pl.ds(pl.multiple_of(i * CHUNK, CHUNK), CHUNK)] = (
            dot_nt(solver_high, low) + dot_nt(solver_low, high)
        ) + dot_nt(solver_high, high)

    def ahead(turn, slot, i):
        if slot == 1:

            @pl.when(turn > 0)
            def _():
                copy(turn - 1).start()

        solve(jnp.maximum(i - 1, 0), 1 - slot % 2)

    def emit(i, half, start, total):
        mixed[half, start : start + SUB, :] = total

    mixed[...] = jnp.zeros_like(mixed)
    run(ahead, emit)
    solve(chunks - 1, (chunks - 1) % 2)
    copy(turns - 1).start()
    for turn in range(turns):
        copy(turn).wait()


def mixer_scratch(neighbours):
    return [
        pltpu.VMEM((2, CHUNK, SUB), jnp.float32),
        *[pltpu.SMEM((neighbours, 1, CHUNK), jnp.int32)] * BUFFERS,
        pltpu.SemaphoreType.DMA((BUFFERS,)),
    ]


def rims_kernel(chunk_of, chunks, *refs):
    state_ref, before_ref, after_ref, near_ref, near_tiles_ref, edge_tiles_ref, *refs = refs
    table_ref, rims_ref, near_out, edge_ref, *refs = refs
    factors, *slots, near_sems, table, field, load_sems, table_sem = refs
    levels, cells = state_ref.shape
    places = [(before_ref, 0, HALO), (state_ref, HALO, cells), (after_ref, HALO + cells, HALO)]
    loads = [
        pltpu.make_async_copy(ref, field.at[:, pl.ds(start, length)], load_sems.at[k])
        for k, (ref, start, length) in enumerate(places)
    ]
    loads.append(pltpu.make_async_copy(near_tiles_ref, near_out, load_sems.at[3]))
    loads.append(pltpu.make_async_copy(edge_tiles_ref, edge_ref, load_sems.at[4]))
    begin, run = mixer(near_ref, edge_ref, table, factors, slots, near_sems, chunk_of, chunks)
    for load in loads:
        load.start()
    begin()
    for load in loads:
        load.wait()
    rest = jnp.zeros((LANES - levels, LANES), jnp.float32)

    def turn_tiles(k, carry):
        width = SUB * LANES
        start = pl.multiple_of(k * width, width)
        block = field[:, pl.ds(start, width)]
        for t in range(SUB):
            tile = jnp.concatenate([block[:, t * LANES : (t + 1) * LANES], rest], axis=0)
            table[pl.ds(pl.multiple_of(start + t * LANES, LANES), LANES), :] = tile.T
        return carry

    lax.fori_loop(0, table.shape[0] // (SUB * LANES), turn_tiles, 0)
    save = pltpu.make_async_copy(table, table_ref, table_sem)
    save.start()

    def emit(i, half, start, total):
        rims_ref[pl.ds(pl.multiple_of(i * CHUNK + start, SUB), SUB), :] = total

    run(lambda turn, slot, i: None, emit)
    save.wait()


def mix_rims(state, before, after, near, near_tiles, edge_tiles, chunk_of, chunks):
    levels, cells = state.shape
    extended = cells + 2 * HALO
    return pl.pallas_call(
        functools.partial(rims_kernel, chunk_of, chunks),
        in_specs=[outside()] + [anywhere()] * 2 + [outside()] * 3,
        out_specs=[outside()] + [whole()] * 3,
        out_shape=[
            pltpu.HBM((extended, LANES), jnp.float32),
            jax.ShapeDtypeStruct((chunks * CHUNK, LANES), jnp.float32),
            pltpu.VMEM(near_tiles.shape, jnp.int32),
            pltpu.VMEM(edge_tiles.shape, jnp.float32),
        ],
        scratch_shapes=mixer_scratch(near.shape[0])
        + [
            pltpu.VMEM((extended, LANES), jnp.float32),
            pltpu.VMEM((levels, extended), jnp.float32),
            pltpu.SemaphoreType.DMA((5,)),
            pltpu.SemaphoreType.DMA,
        ],
        compiler_params=params(16),
        name="mix_rims",
    )(state, before, after, near, near_tiles, edge_tiles)


def low_kernel(chunk_of, chunks, *refs):
    table_ref, rims_ref, near_ref, edge_ref, _, table, next_table, *refs = refs
    factors, *slots, near_sems, load_sems = refs
    last = next_table.shape[0] - 2 * HALO
    places = [
        (table_ref, table),
        (rims_ref.at[pl.ds(0, HALO)], next_table.at[pl.ds(HALO, HALO)]),
        (rims_ref.at[pl.ds(HALO, HALO)], next_table.at[pl.ds(last, HALO)]),
    ]
    loads = [pltpu.make_async_copy(*place, load_sems.at[k]) for k, place in enumerate(places)]
    for load in loads:
        load.start()
    begin, run = mixer(near_ref, edge_ref, table, factors, slots, near_sems, chunk_of, chunks)
    begin()
    for load in loads:
        load.wait()

    def emit(i, half, start, total):
        cell = HALO + chunk_of(i) * CHUNK + start
        next_table[pl.ds(pl.multiple_of(cell, SUB), SUB), :] = total

    run(lambda turn, slot, i: None, emit)


def mix_low(table, rims, near, edges, wait, chunk_of, chunks):
    return pl.pallas_call(
        functools.partial(low_kernel, chunk_of, chunks),
        in_specs=[outside(), anywhere(), outside(), whole(), anywhere()],
        out_specs=[whole()] * 2,
        out_shape=[pltpu.VMEM(table.shape, jnp.float32)] * 2,
        scratch_shapes=mixer_scratch(near.shape[0]) + [pltpu.SemaphoreType.DMA((3,))],
        compiler_params=params(),
        name="mix_low",
    )(table, rims, near, edges, wait)


def high_kernel(chunk_of, chunks, *refs):
    table, _, near_ref, edge_ref, _, next_table, factors, *slots, near_sems = refs
    begin, run = mixer(near_ref, edge_ref, table, factors, slots, near_sems, chunk_of, chunks)
    begin()

    def emit(i, half, start, total):
        cell = HALO + chunk_of(i) * CHUNK + start
        next_table[pl.ds(pl.multiple_of(cell, SUB), SUB), :] = total

    run(lambda turn, slot, i: None, emit)


def mix_high(table, next_table, near, edges, wait, chunk_of, chunks):
    return pl.pallas_call(
        functools.partial(high_kernel, chunk_of, chunks),
        in_specs=[whole()] * 2 + [outside(), whole(), anywhere()],
        out_specs=whole(),
        out_shape=pltpu.VMEM(next_table.shape, jnp.float32),
        input_output_aliases={1: 0},
        scratch_shapes=mixer_scratch(near.shape[0]),
        compiler_params=params(),
        name="mix_high",
    )(table, next_table, near, edges, wait)


def solve_kernel(*refs):
    _, start_ref, end_ref, solver_ref, before_ref, own_ref, after_ref, *refs = refs
    mask_ref, slot_ref, near_ref, edge_ref, *refs = refs
    table, out_ref, surface_ref, payload_ref, *refs = refs
    factors, *slots, near_sems, out_sems, mixed, levels, halo_sems = refs
    chunks = out_ref.shape[1] // CHUNK
    tiles = own_ref.shape[0]
    loads = [
        pltpu.make_async_copy(ref, table.at[pl.ds(start, HALO)], halo_sems.at[k])
        for k, (ref, start) in enumerate([(start_ref, 0), (end_ref, HALO + tiles * LANES)])
    ]
    for load in loads:
        load.start()
    begin, run = mixer(near_ref, edge_ref, table, factors, slots, near_sems, lambda i: i, chunks)
    begin()
    lane = lax.broadcasted_iota(jnp.int32, (LANES, LANES), 1)

    def add_source(source_ref, first, start):
        columns = source_ref[pl.ds(first, SUB), :].T
        for t in range(SUB):
            at = pl.ds(pl.multiple_of(start + t * LANES, LANES), LANES)
            column = jnp.broadcast_to(columns[:, t : t + 1], (LANES, LANES))
            table[at, :] = table[at, :] + jnp.where(lane == 0, column, 0.0)

    def add_own(k, carry):
        first = pl.multiple_of(k * SUB, SUB)
        add_source(own_ref, first, HALO + first * LANES)
        return carry

    lax.fori_loop(0, tiles // SUB, add_own, 0)
    for load in loads:
        load.wait()
    add_source(before_ref, 0, 0)
    add_source(after_ref, 0, HALO + tiles * LANES)
    run_solve(run, chunks, solver_ref, mixed, levels, out_ref, out_sems)

    for k in range(tiles):
        wet = mask_ref[k : k + 1, :].astype(jnp.float32)
        surface_ref[k : k + 1, :] = levels[:1, k * LANES : (k + 1) * LANES] * wet
    owners, slots = slot_ref.shape
    payload_ref[owners:, :] = jnp.zeros((owners, slots), jnp.float32)

    def surface_tile(k):
        return jnp.broadcast_to(surface_ref[k : k + 1, :], (SUB, LANES))

    def pick(group, carry):
        at = pl.ds(pl.multiple_of(group * SUB, SUB), SUB)
        for k in range(slots // LANES):
            cut = slice(k * LANES, (k + 1) * LANES)
            (found,) = pick_lanes(tiles, [surface_tile], slot_ref[at, cut])
            payload_ref[at, cut] = found
        return carry

    lax.fori_loop(0, owners // SUB, pick, 0)


def mix_solve(table, start, end, solver, before, own, after, mask, slots, near, edges):
    cells = own.shape[0] * LANES
    owners, count = slots.shape
    levels = solver.shape[0]
    return pl.pallas_call(
        solve_kernel,
        in_specs=[whole()] + [anywhere()] * 2 + [whole()] * 6 + [outside(), whole()],
        out_specs=[whole(), anywhere(), whole(), whole()],
        out_shape=[
            pltpu.VMEM(table.shape, jnp.float32),
            jax.ShapeDtypeStruct((levels, cells), jnp.float32),
            jax.ShapeDtypeStruct(own.shape, jnp.float32),
            jax.ShapeDtypeStruct((2 * owners, count), jnp.float32),
        ],
        input_output_aliases={0: 0},
        scratch_shapes=mixer_scratch(near.shape[0])
        + [
            pltpu.SemaphoreType.DMA((cells // CHUNK // BUFFERS,)),
            pltpu.VMEM((2, CHUNK, LANES), jnp.float32),
            pltpu.VMEM((levels, cells), jnp.float32),
            pltpu.SemaphoreType.DMA((2,)),
        ],
        compiler_params=params(),
        name="mix_solve",
    )(table, start, end, solver, before, own, after, mask, slots, near, edges)


def to_neighbours(initial, last):
    count = lax.axis_size("blk")
    up = [(i, (i + 1) % count) for i in range(count)]
    down = [(j, i) for i, j in up]
    return lax.ppermute(last, "blk", up), lax.ppermute(initial, "blk", down)


def exchange(array, axes):
    return lax.all_to_all(array, axes, split_axis=0, concat_axis=0, tiled=True)


def shards(
    thermal_profiles,
    adjacent_positions,
    diffusion_link_factor,
    implicit_solver_matrix,
    lagged_surface_temp,
    flux_coefficient,
    flux_heating,
    ocean_cell_mask,
    atmosphere_slot_cells,
    ocean_slot_cells,
    forward_weight_blocks,
    backward_weight_blocks,
):
    ocean = lax.axis_index("comp").astype(jnp.int32).reshape(1)
    state = thermal_profiles[0]
    levels, cells = state.shape
    neighbours = adjacent_positions.shape[1]
    near = far(adjacent_positions.reshape(neighbours, 1, cells))
    tiles = cells // LANES
    mask = ocean_cell_mask.reshape(tiles, LANES)
    atmosphere_slots = atmosphere_slot_cells[0]
    ocean_slots = ocean_slot_cells[0]
    backward_weights = near_by(backward_weight_blocks[0])
    solver = implicit_solver_matrix[0]
    twice = jnp.dot(solver, solver, precision=HIGHEST)
    twice = jnp.pad(twice, ((0, 0), (0, LANES - levels)))

    lowest = state[levels - 1 :]
    flux, payload = pack(
        ocean,
        far(flux_coefficient),
        lowest,
        lax.ppermute(lowest, "comp", [(0, 1)]),
        far(lagged_surface_temp.reshape(1, cells)),
        far(atmosphere_slots),
    )
    arrived = exchange(payload, "blk")

    before, after = to_neighbours(state[:, :HALO], state[:, cells - HALO :])
    rim = HALO // CHUNK
    chunks = cells // CHUNK
    half = (chunks - 2 * rim) // 2
    table, rims, near_tiles, edges = mix_rims(
        far(state),
        before,
        after,
        near,
        far(adjacent_positions.reshape(neighbours, tiles, LANES)),
        far(diffusion_link_factor.reshape(neighbours, tiles, LANES)),
        lambda i: jnp.where(i < rim, i, i + chunks - 2 * rim),
        2 * rim,
    )
    next_before, next_after = to_neighbours(rims[:HALO], rims[HALO:])

    flux_out, source = forward(
        ocean,
        flux_heating,
        far(forward_weight_blocks[0]),
        arrived,
        ocean_slots,
        mask,
        flux,
    )
    rim_rows = HALO // LANES
    source_before, source_after = to_neighbours(source[:rim_rows], source[-rim_rows:])
    table, next_table = mix_low(far(table), rims, near, edges, source, lambda i: i + rim, half)
    mixed = mix_source(source_before, source, source_after, near_tiles, edges, next_table)
    mixed_before, mixed_after = to_neighbours(mixed[:rim_rows], mixed[-rim_rows:])
    next_table = mix_high(
        table, next_table, near, edges, mixed, lambda i: i + rim + half, half
    )
    _, result, surface, back_payload = mix_solve(
        next_table,
        next_before,
        next_after,
        twice,
        mixed_before,
        mixed,
        mixed_after,
        mask,
        ocean_slots,
        near,
        edges,
    )
    warmth = backward(
        ocean,
        backward_weights,
        exchange(back_payload, ("comp", "blk")),
        atmosphere_slots,
        surface,
    )
    return (result[None], flux_out[None], warmth)


def solution(mesh):
    placed = (
        P("comp", None, "blk"),
        P("comp", None, "blk"),
        P("comp", None, "blk"),
        P("comp", None, None),
        P("blk"),
        P(None, "blk"),
        P(),
        P("blk"),
        P("blk", None, None),
        P("blk", None, None),
        P("blk", None, None, None),
        P("blk", None, None, None),
    )
    return jax.shard_map(
        shards,
        mesh=mesh,
        in_specs=placed,
        out_specs=(P("comp", None, "blk"), P("comp", None, "blk"), P("comp", "blk")),
        check_vma=False,
    )
```

```python
import functools

import jax
import jax.numpy as jnp
from jax import lax
from jax.experimental import pallas as pl
from jax.experimental.pallas import tpu as pltpu
from jax.sharding import PartitionSpec as P

HALO = 1024
CHUNK = 256
LANES = 128
WIDE = 256
SUB = 8
BUFFERS = 4
GROUP = 4
HIGHEST = lax.Precision.HIGHEST


def split(value):
    high = value.astype(jnp.bfloat16)
    return high, (value - high.astype(jnp.float32)).astype(jnp.bfloat16)


def dot(a, b):
    return jnp.dot(a, b, preferred_element_type=jnp.float32)


def dot_nt(a, b):
    return lax.dot_general(a, b, (((1,), (1,)), ((), ())), preferred_element_type=jnp.float32)


def params(mebibytes=8):
    return pltpu.CompilerParams(vmem_limit_bytes=mebibytes * 2**20)


def whole():
    return pl.BlockSpec(memory_space=pltpu.VMEM)


def scalars():
    return pl.BlockSpec(memory_space=pltpu.SMEM)


def anywhere():
    return pl.BlockSpec(memory_space=pl.ANY)


def outside():
    return pl.BlockSpec(memory_space=pltpu.HBM)


def far(array):
    return pltpu.with_memory_space_constraint(array, pltpu.HBM)


def near_by(array):
    return pltpu.with_memory_space_constraint(array, pltpu.VMEM)


def lanes_from(row, lane):
    return jnp.take_along_axis(row, lane, axis=1)


def pick_lanes(count, tables, cells, parts=4):
    high, low = cells >> 7, cells & (LANES - 1)
    totals = []
    for part in range(parts):
        found = [jnp.zeros(cells.shape, jnp.float32) for _ in tables]
        for tile in range(part, count, parts):
            here = high == tile
            found = [
                jnp.where(here, lanes_from(table(tile), low), seen)
                for table, seen in zip(tables, found)
            ]
        totals.append(found)
    return [functools.reduce(lambda a, b: a + b, column) for column in zip(*totals)]


def pack_kernel(
    ocean_ref, coefficient_ref, own_ref, received_ref, lagged_ref, slot_ref, flux_ref, payload_ref
):
    fields, cells = coefficient_ref.shape
    for k in range(cells // LANES):
        cut = slice(k * LANES, (k + 1) * LANES)
        air = jnp.where(ocean_ref[0] == 1, received_ref[:, cut], own_ref[:, cut])
        flux_ref[:, cut] = coefficient_ref[:, cut] * (air - lagged_ref[:, cut])
    owners, slots = slot_ref.shape
    width = min(slots, LANES)
    pieces = slots // width

    def tile_of(base, k):
        return flux_ref[base : base + SUB, k * LANES : (k + 1) * LANES]

    tables = [functools.partial(tile_of, base) for base in range(0, fields, SUB)]

    def body(owner, carry):
        row = slot_ref[pl.ds(owner, 1), :]
        for piece in range(pieces):
            where = row[:, piece * width : (piece + 1) * width]
            if width < LANES:
                where = jnp.concatenate([where] * (LANES // width), axis=1)
            where = jnp.broadcast_to(where, (SUB, LANES))
            for n, found in enumerate(pick_lanes(cells // LANES, tables, where)):
                payload_ref[owner, n * SUB : (n + 1) * SUB, piece * width : (piece + 1) * width] = (
                    found[:, :width]
                )
        return carry

    lax.fori_loop(0, owners, body, 0, unroll=2)


def pack(ocean, coefficient, own, received, lagged, slots):
    fields, cells = coefficient.shape
    owners, count = slots.shape
    return pl.pallas_call(
        pack_kernel,
        in_specs=[scalars()] + [whole()] * 5,
        out_specs=[whole()] * 2,
        out_shape=[
            pltpu.VMEM((fields, cells), jnp.float32),
            jax.ShapeDtypeStruct((owners, fields, count), jnp.float32),
        ],
        compiler_params=params(),
        name="pack",
    )(ocean, coefficient, own, received, lagged, slots)


def row_of(ref, k, width):
    tiles = width // LANES
    return jnp.concatenate([ref[k * tiles + t : k * tiles + t + 1, :] for t in range(tiles)], axis=1)


def one_of(low):
    shape = WIDE, low.shape[1]
    row = lax.broadcasted_iota(jnp.int32, shape, 0).astype(jnp.float32).astype(jnp.bfloat16)
    low = jnp.broadcast_to(low.astype(jnp.float32).astype(jnp.bfloat16), shape)
    return jnp.where(row == low, jnp.bfloat16(1.0), jnp.bfloat16(0.0))


def forward_kernel(
    ocean_ref, heat_ref, weight_ref, arrived_ref, slot_ref, mask_ref, flux_ref, out_ref, source_ref,
    held, total, sems,
):
    owners, fields, _ = arrived_ref.shape
    slots = slot_ref.shape[1]
    highs = total.shape[0] // fields

    def fetch(k):
        return pltpu.make_async_copy(weight_ref.at[k], held.at[k], sems.at[k])

    for k in range(owners):
        fetch(k).start()
    total[...] = jnp.zeros_like(total)
    zero = jnp.zeros((fields, slots), jnp.bfloat16)

    def added(k):
        value_high, value_low = split(arrived_ref[k])
        weight_high, weight_low = split(held[k])
        both = dot_nt(jnp.concatenate([value_high, value_low], axis=0), weight_high)
        mapped = (both[fields:] + dot_nt(value_high, weight_low)) + both[:fields]
        parts = split(mapped)
        cell = slot_ref[pl.ds(k, 1), :]
        high = jnp.broadcast_to(cell >> 8, (fields, slots)).astype(jnp.float32)
        high = high.astype(jnp.bfloat16)
        spread = one_of(cell & (WIDE - 1))
        here = [high == jnp.bfloat16(h) for h in range(highs)]
        rows = [
            jnp.concatenate([jnp.where(here[h], part, zero) for h in range(highs)], axis=0)
            for part in parts
        ]
        return dot_nt(rows[1], spread) + dot_nt(rows[0], spread)

    def body(turn, carry):
        for k in range(GROUP):
            fetch(turn * GROUP + k).wait()
        parts = [added(turn * GROUP + k) for k in range(GROUP)]
        total[...] += functools.reduce(lambda a, b: a + b, parts)
        return carry

    lax.fori_loop(0, owners // GROUP, body, 0)
    ocean = ocean_ref[0]
    sub = lax.broadcasted_iota(jnp.int32, (fields, WIDE), 0)
    heat = jnp.zeros((fields, WIDE), jnp.float32)
    for f in range(fields):
        heat = jnp.where(sub == f, heat_ref[f], heat)
    for h in range(highs):
        cut = slice(h * WIDE, (h + 1) * WIDE)
        wet = row_of(mask_ref, h, WIDE).astype(jnp.float32)
        block = total[h * fields : (h + 1) * fields, :] * wet
        out_ref[:, cut] = jnp.where(ocean == 1, block, flux_ref[:, cut])
        source = jnp.sum(heat * block, axis=0, keepdims=True)
        source = jnp.where(ocean == 1, source, 0.0)
        for t in range(WIDE // LANES):
            at = h * (WIDE // LANES) + t
            source_ref[at : at + 1, :] = source[:, t * LANES : (t + 1) * LANES]


def forward(ocean, heating, weights, arrived, slots, mask, flux):
    owners, fields, _ = arrived.shape
    cells = flux.shape[1]
    return pl.pallas_call(
        forward_kernel,
        in_specs=[scalars()] * 2 + [outside()] + [whole()] * 4,
        out_specs=[whole()] * 2,
        out_shape=[
            jax.ShapeDtypeStruct((fields, cells), jnp.float32),
            jax.ShapeDtypeStruct((cells // LANES, LANES), jnp.float32),
        ],
        scratch_shapes=[
            pltpu.VMEM(weights.shape, jnp.float32),
            pltpu.VMEM((cells // WIDE * fields, WIDE), jnp.float32),
            pltpu.SemaphoreType.DMA((owners,)),
        ],
        compiler_params=params(24),
        name="forward",
    )(ocean, heating, weights, arrived, slots, mask, flux)


def mix_source_kernel(before_ref, own_ref, after_ref, near_ref, edge_ref, _, out_ref):
    tiles = own_ref.shape[0]
    rim = before_ref.shape[0]
    neighbours = near_ref.shape[0]

    def tile_of(k):
        if k < rim:
            row = before_ref[k : k + 1, :]
        elif k < rim + tiles:
            row = own_ref[k - rim : k - rim + 1, :]
        else:
            row = after_ref[k - rim - tiles : k - rim - tiles + 1, :]
        return jnp.broadcast_to(row, (SUB, LANES))

    def body(group, carry):
        at = pl.ds(pl.multiple_of(group * SUB, SUB), SUB)
        keep = jnp.ones((SUB, LANES), jnp.float32)
        total = jnp.zeros((SUB, LANES), jnp.float32)
        for j in range(neighbours):
            edge = edge_ref[j, at, :]
            (found,) = pick_lanes(tiles + 2 * rim, [tile_of], near_ref[j, at, :])
            total = total + edge * found
            keep = keep - edge
        out_ref[at, :] = total + keep * own_ref[at, :]
        return carry

    lax.fori_loop(0, tiles // SUB, body, 0)


def mix_source(before, own, after, near, edges, wait):
    return pl.pallas_call(
        mix_source_kernel,
        in_specs=[whole()] * 5 + [anywhere()],
        out_specs=whole(),
        out_shape=jax.ShapeDtypeStruct(own.shape, jnp.float32),
        compiler_params=params(),
        name="mix_source",
    )(before, own, after, near, edges, wait)


def backward_kernel(
    ocean_ref, weight_ref, arrived_ref, slot_ref, surface_ref, out_ref, total
):
    owners, slots = slot_ref.shape
    highs = total.shape[0]
    total[...] = jnp.zeros_like(total)

    def added(k):
        weight_high, weight_low = split(weight_ref[k])
        value = arrived_ref[pl.ds(owners + k, 1), :]
        value = jnp.broadcast_to(value, (2 * SUB, value.shape[1]))
        value_high, value_low = split(value)
        mapped = (dot_nt(value_low, weight_high) + dot_nt(value_high, weight_low)) + dot_nt(
            value_high, weight_high
        )
        mapped = jnp.broadcast_to(mapped[:1], (highs, slots))
        cell = slot_ref[pl.ds(k, 1), :]
        high = jnp.broadcast_to(cell >> 8, (highs, slots))
        spread = one_of(cell & (WIDE - 1))
        here = lax.broadcasted_iota(jnp.int32, (highs, slots), 0) == high
        part_high, part_low = split(jnp.where(here, mapped, 0.0))
        return dot_nt(part_low, spread) + dot_nt(part_high, spread)

    def body(turn, carry):
        parts = [added(turn * GROUP + k) for k in range(GROUP)]
        total[...] += functools.reduce(lambda a, b: a + b, parts)
        return carry

    lax.fori_loop(0, owners // GROUP, body, 0)
    for h in range(highs):
        row = jnp.where(ocean_ref[0] == 1, row_of(surface_ref, h, WIDE), total[h : h + 1, :])
        out_ref[:, h * WIDE : (h + 1) * WIDE] = row


def backward(ocean, weights, arrived, slots, surface):
    owners, _ = slots.shape
    cells = surface.shape[0] * LANES
    return pl.pallas_call(
        backward_kernel,
        in_specs=[scalars()] + [whole()] * 4,
        out_specs=whole(),
        out_shape=jax.ShapeDtypeStruct((1, cells), jnp.float32),
        scratch_shapes=[
            pltpu.VMEM((cells // WIDE, WIDE), jnp.float32),
        ],
        compiler_params=params(),
        name="backward",
    )(ocean, weights, arrived, slots, surface)


def mixer(near_ref, edge_ref, table, factors, slots, near_sems, chunk_of, chunks):
    neighbours = near_ref.shape[0]

    def fetch(i, slot):
        start = pl.multiple_of(chunk_of(i) * CHUNK, CHUNK)
        return pltpu.make_async_copy(
            near_ref.at[:, :, pl.ds(start, CHUNK)], slots[slot], near_sems.at[slot]
        )

    def begin():
        for slot in range(BUFFERS - 1):
            fetch(slot, slot).start()

    def set_factors(i, half):
        tiles = CHUNK // LANES
        edges = [
            jnp.concatenate(
                [edge_ref[j, pl.ds(chunk_of(i) * tiles + t, 1), :] for t in range(tiles)], axis=1
            )
            for j in range(neighbours)
        ]
        keep = 1.0 - functools.reduce(lambda a, b: a + b, edges)
        rest = jnp.zeros((SUB - neighbours - 1, CHUNK), jnp.float32)
        factors[half] = jnp.concatenate(edges + [keep, rest], axis=0).T

    def run(ahead, emit):
        set_factors(0, 0)
        sub = lax.broadcasted_iota(jnp.int32, (SUB, LANES), 0)
        masks = [sub == s for s in range(SUB)]

        def body(turn, carry):
            for slot in range(BUFFERS):
                i = turn * BUFFERS + slot
                half = slot % 2
                fetch(i, slot).wait()

                @pl.when(i + BUFFERS - 1 < chunks)
                def _():
                    fetch(i + BUFFERS - 1, (slot + BUFFERS - 1) % BUFFERS).start()

                ahead(turn, slot, i)
                set_factors(jnp.minimum(i + 1, chunks - 1), 1 - half)
                cell = pl.multiple_of(chunk_of(i) * CHUNK, CHUNK)
                for g in range(CHUNK // SUB):
                    own = table[pl.ds(pl.multiple_of(HALO + cell + g * SUB, SUB), SUB), :]
                    part = factors[half, g * SUB : (g + 1) * SUB, :]
                    total = own * jnp.broadcast_to(
                        part[:, neighbours : neighbours + 1], (SUB, LANES)
                    )
                    for j in range(neighbours):
                        picked = None
                        for s in range(SUB):
                            where = slots[slot][j, 0, g * SUB + s]
                            row = jnp.broadcast_to(table[pl.ds(where, 1), :], (SUB, LANES))
                            picked = row if s == 0 else jnp.where(masks[s], row, picked)
                        total = total + jnp.broadcast_to(part[:, j : j + 1], (SUB, LANES)) * picked
                    emit(i, half, g * SUB, total)
            return carry

        lax.fori_loop(0, chunks // BUFFERS, body, 0)

    return begin, run


def run_solve(run, chunks, solver_ref, mixed, levels, out_ref, out_sems):
    length = BUFFERS * CHUNK
    turns = chunks // BUFFERS

    def copy(turn):
        at = pl.ds(pl.multiple_of(turn * length, length), length)
        return pltpu.make_async_copy(levels.at[:, at], out_ref.at[:, at], out_sems.at[turn])

    def solve(i, half):
        high, low = split(mixed[half])
        solver_high, solver_low = split(solver_ref[...])
        levels[:, pl.ds(pl.multiple_of(i * CHUNK, CHUNK), CHUNK)] = (
            dot_nt(solver_high, low) + dot_nt(solver_low, high)
        ) + dot_nt(solver_high, high)

    def ahead(turn, slot, i):
        if slot == 1:

            @pl.when(turn > 0)
            def _():
                copy(turn - 1).start()

        solve(jnp.maximum(i - 1, 0), 1 - slot % 2)

    def emit(i, half, start, total):
        mixed[half, start : start + SUB, :] = total

    mixed[...] = jnp.zeros_like(mixed)
    run(ahead, emit)
    solve(chunks - 1, (chunks - 1) % 2)
    copy(turns - 1).start()
    for turn in range(turns):
        copy(turn).wait()


def mixer_scratch(neighbours):
    return [
        pltpu.VMEM((2, CHUNK, SUB), jnp.float32),
        *[pltpu.SMEM((neighbours, 1, CHUNK), jnp.int32)] * BUFFERS,
        pltpu.SemaphoreType.DMA((BUFFERS,)),
    ]


def rims_kernel(chunk_of, chunks, *refs):
    state_ref, before_ref, after_ref, near_ref, near_tiles_ref, edge_tiles_ref, *refs = refs
    table_ref, rims_ref, near_out, edge_ref, *refs = refs
    factors, *slots, near_sems, table, field, load_sems, table_sem = refs
    levels, cells = state_ref.shape
    places = [(before_ref, 0, HALO), (state_ref, HALO, cells), (after_ref, HALO + cells, HALO)]
    loads = [
        pltpu.make_async_copy(ref, field.at[:, pl.ds(start, length)], load_sems.at[k])
        for k, (ref, start, length) in enumerate(places)
    ]
    loads.append(pltpu.make_async_copy(near_tiles_ref, near_out, load_sems.at[3]))
    loads.append(pltpu.make_async_copy(edge_tiles_ref, edge_ref, load_sems.at[4]))
    begin, run = mixer(near_ref, edge_ref, table, factors, slots, near_sems, chunk_of, chunks)
    for load in loads:
        load.start()
    begin()
    for load in loads:
        load.wait()
    rest = jnp.zeros((LANES - levels, LANES), jnp.float32)

    def turn_tiles(k, carry):
        width = SUB * LANES
        start = pl.multiple_of(k * width, width)
        block = field[:, pl.ds(start, width)]
        for t in range(SUB):
            tile = jnp.concatenate([block[:, t * LANES : (t + 1) * LANES], rest], axis=0)
            table[pl.ds(pl.multiple_of(start + t * LANES, LANES), LANES), :] = tile.T
        return carry

    lax.fori_loop(0, table.shape[0] // (SUB * LANES), turn_tiles, 0)
    save = pltpu.make_async_copy(table, table_ref, table_sem)
    save.start()

    def emit(i, half, start, total):
        rims_ref[pl.ds(pl.multiple_of(i * CHUNK + start, SUB), SUB), :] = total

    run(lambda turn, slot, i: None, emit)
    save.wait()


def mix_rims(state, before, after, near, near_tiles, edge_tiles, chunk_of, chunks):
    levels, cells = state.shape
    extended = cells + 2 * HALO
    return pl.pallas_call(
        functools.partial(rims_kernel, chunk_of, chunks),
        in_specs=[outside()] + [anywhere()] * 2 + [outside()] * 3,
        out_specs=[outside()] + [whole()] * 3,
        out_shape=[
            pltpu.HBM((extended, LANES), jnp.float32),
            jax.ShapeDtypeStruct((chunks * CHUNK, LANES), jnp.float32),
            pltpu.VMEM(near_tiles.shape, jnp.int32),
            pltpu.VMEM(edge_tiles.shape, jnp.float32),
        ],
        scratch_shapes=mixer_scratch(near.shape[0])
        + [
            pltpu.VMEM((extended, LANES), jnp.float32),
            pltpu.VMEM((levels, extended), jnp.float32),
            pltpu.SemaphoreType.DMA((5,)),
            pltpu.SemaphoreType.DMA,
        ],
        compiler_params=params(16),
        name="mix_rims",
    )(state, before, after, near, near_tiles, edge_tiles)


def low_kernel(chunk_of, chunks, *refs):
    table_ref, rims_ref, near_ref, edge_ref, _, table, next_table, *refs = refs
    factors, *slots, near_sems, load_sems = refs
    last = next_table.shape[0] - 2 * HALO
    places = [
        (table_ref, table),
        (rims_ref.at[pl.ds(0, HALO)], next_table.at[pl.ds(HALO, HALO)]),
        (rims_ref.at[pl.ds(HALO, HALO)], next_table.at[pl.ds(last, HALO)]),
    ]
    loads = [pltpu.make_async_copy(*place, load_sems.at[k]) for k, place in enumerate(places)]
    for load in loads:
        load.start()
    begin, run = mixer(near_ref, edge_ref, table, factors, slots, near_sems, chunk_of, chunks)
    begin()
    for load in loads:
        load.wait()

    def emit(i, half, start, total):
        cell = HALO + chunk_of(i) * CHUNK + start
        next_table[pl.ds(pl.multiple_of(cell, SUB), SUB), :] = total

    run(lambda turn, slot, i: None, emit)


def mix_low(table, rims, near, edges, wait, chunk_of, chunks):
    return pl.pallas_call(
        functools.partial(low_kernel, chunk_of, chunks),
        in_specs=[outside(), anywhere(), outside(), whole(), anywhere()],
        out_specs=[whole()] * 2,
        out_shape=[pltpu.VMEM(table.shape, jnp.float32)] * 2,
        scratch_shapes=mixer_scratch(near.shape[0]) + [pltpu.SemaphoreType.DMA((3,))],
        compiler_params=params(),
        name="mix_low",
    )(table, rims, near, edges, wait)


def high_kernel(chunk_of, chunks, *refs):
    table, _, near_ref, edge_ref, _, next_table, factors, *slots, near_sems = refs
    begin, run = mixer(near_ref, edge_ref, table, factors, slots, near_sems, chunk_of, chunks)
    begin()

    def emit(i, half, start, total):
        cell = HALO + chunk_of(i) * CHUNK + start
        next_table[pl.ds(pl.multiple_of(cell, SUB), SUB), :] = total

    run(lambda turn, slot, i: None, emit)


def mix_high(table, next_table, near, edges, wait, chunk_of, chunks):
    return pl.pallas_call(
        functools.partial(high_kernel, chunk_of, chunks),
        in_specs=[whole()] * 2 + [outside(), whole(), anywhere()],
        out_specs=whole(),
        out_shape=pltpu.VMEM(next_table.shape, jnp.float32),
        input_output_aliases={1: 0},
        scratch_shapes=mixer_scratch(near.shape[0]),
        compiler_params=params(),
        name="mix_high",
    )(table, next_table, near, edges, wait)


def solve_kernel(*refs):
    _, start_ref, end_ref, solver_ref, before_ref, own_ref, after_ref, *refs = refs
    mask_ref, slot_ref, near_ref, edge_ref, *refs = refs
    table, out_ref, surface_ref, payload_ref, *refs = refs
    factors, *slots, near_sems, out_sems, mixed, levels, halo_sems = refs
    chunks = out_ref.shape[1] // CHUNK
    tiles = own_ref.shape[0]
    count = solver_ref.shape[0]
    last = HALO + tiles * LANES
    places = [(start_ref, table.at[pl.ds(0, HALO)]), (end_ref, table.at[pl.ds(last, HALO)])]
    loads = [pltpu.make_async_copy(*place, halo_sems.at[k]) for k, place in enumerate(places)]
    for load in loads:
        load.start()
    begin, run = mixer(near_ref, edge_ref, table, factors, slots, near_sems, lambda i: i, chunks)
    begin()
    lane = lax.broadcasted_iota(jnp.int32, (LANES, LANES), 1)

    def add_source(source, start):
        block = [
            jnp.zeros((count, LANES), jnp.float32),
            source,
            jnp.zeros((LANES - count - SUB, LANES), jnp.float32),
        ]
        columns = jnp.concatenate(block, axis=0).T
        for t in range(SUB):
            at = pl.ds(pl.multiple_of(start + t * LANES, LANES), LANES)
            table[at, :] = table[at, :] + jnp.where(lane == count + t, columns, 0.0)

    def add_own(k, carry):
        first = pl.multiple_of(k * SUB, SUB)
        add_source(own_ref[pl.ds(first, SUB), :], HALO + first * LANES)
        return carry

    lax.fori_loop(0, tiles // SUB, add_own, 0)
    for load in loads:
        load.wait()
    add_source(before_ref[...], 0)
    add_source(after_ref[...], last)
    run_solve(run, chunks, solver_ref, mixed, levels, out_ref, out_sems)

    for k in range(tiles):
        wet = mask_ref[k : k + 1, :].astype(jnp.float32)
        surface_ref[k : k + 1, :] = levels[:1, k * LANES : (k + 1) * LANES] * wet
    owners, slots = slot_ref.shape
    payload_ref[owners:, :] = jnp.zeros((owners, slots), jnp.float32)

    def surface_tile(k):
        return jnp.broadcast_to(surface_ref[k : k + 1, :], (SUB, LANES))

    def pick(group, carry):
        at = pl.ds(pl.multiple_of(group * SUB, SUB), SUB)
        for k in range(slots // LANES):
            cut = slice(k * LANES, (k + 1) * LANES)
            (found,) = pick_lanes(tiles, [surface_tile], slot_ref[at, cut])
            payload_ref[at, cut] = found
        return carry

    lax.fori_loop(0, owners // SUB, pick, 0)


def mix_solve(table, start, end, solver, before, own, after, mask, slots, near, edges):
    cells = own.shape[0] * LANES
    owners, count = slots.shape
    levels = solver.shape[0]
    return pl.pallas_call(
        solve_kernel,
        in_specs=[whole()] + [anywhere()] * 2 + [whole()] * 6 + [outside(), whole()],
        out_specs=[whole(), anywhere(), whole(), whole()],
        out_shape=[
            pltpu.VMEM(table.shape, jnp.float32),
            jax.ShapeDtypeStruct((levels, cells), jnp.float32),
            jax.ShapeDtypeStruct(own.shape, jnp.float32),
            jax.ShapeDtypeStruct((2 * owners, count), jnp.float32),
        ],
        input_output_aliases={0: 0},
        scratch_shapes=mixer_scratch(near.shape[0])
        + [
            pltpu.SemaphoreType.DMA((cells // CHUNK // BUFFERS,)),
            pltpu.VMEM((2, CHUNK, LANES), jnp.float32),
            pltpu.VMEM((levels, cells), jnp.float32),
            pltpu.SemaphoreType.DMA((2,)),
        ],
        compiler_params=params(),
        name="mix_solve",
    )(table, start, end, solver, before, own, after, mask, slots, near, edges)


def to_neighbours(initial, last):
    count = lax.axis_size("blk")
    up = [(i, (i + 1) % count) for i in range(count)]
    down = [(j, i) for i, j in up]
    return lax.ppermute(last, "blk", up), lax.ppermute(initial, "blk", down)


def exchange(array, axes):
    return lax.all_to_all(array, axes, split_axis=0, concat_axis=0, tiled=True)


def shards(
    thermal_profiles,
    adjacent_positions,
    diffusion_link_factor,
    implicit_solver_matrix,
    lagged_surface_temp,
    flux_coefficient,
    flux_heating,
    ocean_cell_mask,
    atmosphere_slot_cells,
    ocean_slot_cells,
    forward_weight_blocks,
    backward_weight_blocks,
):
    ocean = lax.axis_index("comp").astype(jnp.int32).reshape(1)
    state = thermal_profiles[0]
    levels, cells = state.shape
    neighbours = adjacent_positions.shape[1]
    near = far(adjacent_positions.reshape(neighbours, 1, cells))
    tiles = cells // LANES
    mask = ocean_cell_mask.reshape(tiles, LANES)
    atmosphere_slots = atmosphere_slot_cells[0]
    ocean_slots = ocean_slot_cells[0]
    backward_weights = near_by(backward_weight_blocks[0])
    solver = implicit_solver_matrix[0]
    twice = jnp.dot(solver, solver, precision=HIGHEST)
    twice = jnp.concatenate(
        [
            twice,
            jnp.broadcast_to(twice[:, :1], (levels, SUB)),
            jnp.zeros((levels, LANES - levels - SUB), jnp.float32),
        ],
        axis=1,
    )

    lowest = state[levels - 1 :]
    flux, payload = pack(
        ocean,
        far(flux_coefficient),
        lowest,
        lax.ppermute(lowest, "comp", [(0, 1)]),
        far(lagged_surface_temp.reshape(1, cells)),
        far(atmosphere_slots),
    )
    arrived = exchange(payload, "blk")

    before, after = to_neighbours(state[:, :HALO], state[:, cells - HALO :])
    rim = HALO // CHUNK
    chunks = cells // CHUNK
    few = (chunks - 2 * rim) // 2
    table, rims, near_tiles, edges = mix_rims(
        far(state),
        before,
        after,
        near,
        far(adjacent_positions.reshape(neighbours, tiles, LANES)),
        far(diffusion_link_factor.reshape(neighbours, tiles, LANES)),
        lambda i: jnp.where(i < rim, i, i + chunks - 2 * rim),
        2 * rim,
    )

    next_before, next_after = to_neighbours(rims[:HALO], rims[HALO:])

    flux_out, source = forward(
        ocean,
        flux_heating,
        far(forward_weight_blocks[0]),
        arrived,
        ocean_slots,
        mask,
        flux,
    )
    rim_rows = HALO // LANES
    source_before, source_after = to_neighbours(source[:rim_rows], source[-rim_rows:])
    table, next_table = mix_low(far(table), rims, near, edges, source, lambda i: i + rim, few)
    mixed = mix_source(source_before, source, source_after, near_tiles, edges, next_table)
    mixed_before, mixed_after = to_neighbours(mixed[:rim_rows], mixed[-rim_rows:])
    next_table = mix_high(
        table,
        next_table,
        near,
        edges,
        mixed,
        lambda i: i + rim + few,
        chunks - 2 * rim - few,
    )
    _, result, surface, back_payload = mix_solve(
        next_table,
        next_before,
        next_after,
        twice,
        mixed_before,
        mixed,
        mixed_after,
        mask,
        ocean_slots,
        near,
        edges,
    )
    warmth = backward(
        ocean,
        backward_weights,
        exchange(back_payload, ("comp", "blk")),
        atmosphere_slots,
        surface,
    )
    return (result[None], flux_out[None], warmth)


def solution(mesh):
    placed = (
        P("comp", None, "blk"),
        P("comp", None, "blk"),
        P("comp", None, "blk"),
        P("comp", None, None),
        P("blk"),
        P(None, "blk"),
        P(),
        P("blk"),
        P("blk", None, None),
        P("blk", None, None),
        P("blk", None, None, None),
        P("blk", None, None, None),
    )
    return jax.shard_map(
        shards,
        mesh=mesh,
        in_specs=placed,
        out_specs=(P("comp", None, "blk"), P("comp", None, "blk"), P("comp", "blk")),
        check_vma=False,
    )
```
